256 devices in a mesh: quad: 8 (over z_lo, core), dom: 32 (over x, y, z_hi).
Axes of the slice: x: 4, y: 4, z: 8 (z_hi: 2, z_lo: 4; z = z_hi * 4 + z_lo), core: 2. Of those that a mesh axis runs over, the one named last changes fastest.
Arguments:
- probes: float32 [2, 64, 256, 128], P(None, None, 'dom'), may hold values from -6 to 6
- mass_weights: float32 [256, 128], P('dom'), may hold values from 0.8 to 1.25
- blocks: float32 [2, 256, 128, 128], P(None, 'dom'), may hold values from -4 to 4
- couplings: float32 [2, 6, 256, 128], P(None, None, 'dom'), may hold values from -0.25 to 0.25
Outputs:
- moments: float32 [64, 4, 2, 256, 128], P('quad', None, None, 'dom')
- projected: float32 [2, 8, 64, 64], replicated
The draws below stay inside these ranges and needn't reach their ends.
All inputs are finite; a program needn't handle non-finite values.
Results may differ from the reference program's by a relative error of at most 0.0001.
Values sent between devices are 32-bit elements; how exact they have to be, the bound alone decides.
A program may use at most 64 MiB of HBM per device.

```python
import math
import jax
import jax.numpy as jnp
from jax import lax

NY = 128
PROBES = 64
NQ = 16
ITERS = 4
MOM = 4
NX = 256


def draw_blocks(key, part):
    key_off, key_side, key_radius, key_angle = jax.random.split(jax.random.fold_in(key, 7), 4)
    offdiag = jax.random.uniform(key_off, (2, NX, NY, NY), jnp.float32, -1.0, 1.0) * (0.25 / math.sqrt(NY))
    inside = jax.random.bernoulli(key_side, 0.5, (NX, NY)).astype(jnp.float32)
    unit = jax.random.uniform(key_radius, (NX, NY), jnp.float32, 0.0, 1.0)
    radius = inside * (0.75 * unit) + (1.0 - inside) * (3.4 + 0.6 * unit)
    angle = jax.random.uniform(key_angle, (NX, NY), jnp.float32, -math.pi, math.pi)
    diagonal = jnp.stack([radius * jnp.cos(angle), radius * jnp.sin(angle)])
    on_diagonal = jnp.arange(NY)[:, None] == jnp.arange(NY)[None, :]
    return jnp.where(on_diagonal[None, None], diagonal[:, :, :, None], offdiag)


def steps_of(stream_key, shape, pieces, smallest, high):
    loudness, own = 1.0, jax.random.fold_in(stream_key, 6)
    for dim, parts in pieces:
        steps = jnp.exp(jax.random.uniform(jax.random.fold_in(own, dim), (parts,), jnp.float32, smallest / len(pieces), high / len(pieces)))
        loudness = loudness * jnp.repeat(steps, shape[dim] // parts).reshape([-1 if axis == dim else 1 for axis in range(len(shape))])
    return loudness


def bell_draw(key, shape, width, reach, shards=(), held_as=jnp.bfloat16):
    array = jax.random.normal(key, shape, jnp.float32) * width
    if len(shards) > 0:
        array = steps_of(key, shape, shards, -0.22, 0.18) * array
    return jnp.clip(array, min=-reach, max=reach).astype(held_as)


def setup_inputs(seed: int = 0) -> dict:
    splits = jax.random.split(jax.random.key(seed), 5)
    probes = bell_draw(splits[0], (2, PROBES, NX, NY), 1.0, 6.0, ((2, 32),), jnp.float32)
    mass_weights = jnp.clip(jnp.exp(math.log(1.25) - 0.4462871 * jax.random.uniform(splits[1], (NX, NY), jnp.float32) ** steps_of(splits[1], (NX, NY), ((0, 32),), -0.2, 0.2)), 0.8, 1.25)
    blocks = draw_blocks(jax.random.fold_in(splits[4], 71), 0)
    couplings = jnp.clip(jax.random.uniform(splits[3], (2, 6, NX, NY), jnp.float32, -0.25, 0.25) * steps_of(splits[3], (2, 6, NX, NY), ((2, 32),), -0.4, 0.0), -0.25, 0.25)
    return dict(probes=probes, mass_weights=mass_weights, blocks=blocks, couplings=couplings)


PRECISE = lax.Precision.HIGHEST
RADIUS = 2.0
OFFSETS = (-3, -2, -1, 1, 2, 3)


def shift_angles(shift_index, total_shifts):
    return (2.0 * math.pi / total_shifts) * (shift_index.astype(jnp.float32) + 0.5)


def moment_weights(angles, moment_count, scale):
    orders = jnp.arange(1, moment_count + 1, dtype=jnp.float32)
    phases = orders[:, None] * angles[None, :]
    return scale * jnp.cos(phases), scale * jnp.sin(phases)


def sweep(field, padded, blocks, couplings, zmass_re, zmass_im, inverse_re, inverse_im, source):
    rim_depth = max(OFFSETS)
    line_count = field.shape[3]
    field_re = field[0]
    field_im = field[1]
    image_re = jnp.einsum("spxj,xij->spxi", field_re, blocks[0], precision=PRECISE) - jnp.einsum("spxj,xij->spxi", field_im, blocks[1], precision=PRECISE)
    image_im = jnp.einsum("spxj,xij->spxi", field_im, blocks[0], precision=PRECISE) + jnp.einsum("spxj,xij->spxi", field_re, blocks[1], precision=PRECISE)
    for position, offset in enumerate(OFFSETS):
        neighbour = padded[:, :, :, rim_depth + offset:rim_depth + offset + line_count]
        coup_re = couplings[0, position]
        coup_im = couplings[1, position]
        image_re = image_re + coup_re * neighbour[0] - coup_im * neighbour[1]
        image_im = image_im + coup_re * neighbour[1] + coup_im * neighbour[0]
    resid_re = source[0] - (zmass_re * field_re - zmass_im * field_im) + image_re
    resid_im = source[1] - (zmass_re * field_im + zmass_im * field_re) + image_im
    return jnp.stack([field_re + resid_re * inverse_re - resid_im * inverse_im,
                      field_im + resid_re * inverse_im + resid_im * inverse_re])


def moment_block(field_part, weight_re, weight_im):
    sum_re = jnp.einsum("ks,spxi->pkxi", weight_re, field_part[0], precision=PRECISE) - jnp.einsum("ks,spxi->pkxi", weight_im, field_part[1], precision=PRECISE)
    sum_im = jnp.einsum("ks,spxi->pkxi", weight_re, field_part[1], precision=PRECISE) + jnp.einsum("ks,spxi->pkxi", weight_im, field_part[0], precision=PRECISE)
    return jnp.stack([sum_re, sum_im], axis=2)


def reference(probes, mass_weights, blocks, couplings):
    rim_depth = max(OFFSETS)
    total_lines = mass_weights.shape[0]
    row_width = mass_weights.shape[1]
    diagonal = jnp.diagonal(blocks, axis1=2, axis2=3)
    source = mass_weights[None, None] * probes
    moments = jnp.zeros((PROBES, MOM, 2, total_lines, row_width), jnp.float32)
    projected = jnp.zeros((2, 2 * MOM, PROBES, PROBES), jnp.float32)
    for shift in range(NQ):
        angles = shift_angles(jnp.full((1,), shift, jnp.int32), NQ)
        zmass_re = (RADIUS * jnp.cos(angles))[:, None, None, None] * mass_weights[None, None]
        zmass_im = (RADIUS * jnp.sin(angles))[:, None, None, None] * mass_weights[None, None]
        denom_re = zmass_re - diagonal[0]
        denom_im = zmass_im - diagonal[1]
        modulus = denom_re * denom_re + denom_im * denom_im
        inverse_re = denom_re / modulus
        inverse_im = -denom_im / modulus
        field = jnp.stack([source[0] * inverse_re - source[1] * inverse_im,
                           source[0] * inverse_im + source[1] * inverse_re])
        for step in range(ITERS - 1):
            padded = jnp.pad(field, ((0, 0), (0, 0), (0, 0), (rim_depth, rim_depth), (0, 0)))
            field = sweep(field, padded, blocks, couplings, zmass_re, zmass_im, inverse_re, inverse_im, source)
        weight_re, weight_im = moment_weights(angles, MOM, RADIUS / NQ)
        moments = moments + moment_block(field, weight_re, weight_im)
        gram_re = jnp.einsum("pxi,sqxi->spq", probes[0], field[0], precision=PRECISE) + jnp.einsum("pxi,sqxi->spq", probes[1], field[1], precision=PRECISE)
        gram_im = jnp.einsum("pxi,sqxi->spq", probes[0], field[1], precision=PRECISE) - jnp.einsum("pxi,sqxi->spq", probes[1], field[0], precision=PRECISE)
        proj_re, proj_im = moment_weights(angles, 2 * MOM, RADIUS / (NQ * total_lines * row_width))
        mixed_re = jnp.einsum("ks,spq->kpq", proj_re, gram_re, precision=PRECISE) - jnp.einsum("ks,spq->kpq", proj_im, gram_im, precision=PRECISE)
        mixed_im = jnp.einsum("ks,spq->kpq", proj_re, gram_im, precision=PRECISE) + jnp.einsum("ks,spq->kpq", proj_im, gram_re, precision=PRECISE)
        projected = projected + jnp.stack([mixed_re, mixed_im])
    return moments, projected
```

```python
import functools
import math

import jax
import jax.numpy as jnp
import numpy as np
from jax import lax
from jax.experimental import pallas as pl
from jax.experimental.pallas import tpu as pltpu
from jax.sharding import PartitionSpec as P

NQ = 16
MOM = 4
RADIUS = 2.0
OFFSETS = (-3, -2, -1, 1, 2, 3)
LINES = 8
OWNED = 8
NY = 128
FIRST = 9
SPAN = 26
ORDER = (7, 0, 6, 1, 5, 4, 2, 3)
RIM = 6
NT = (((1,), (1,)), ((), ()))


def weights():
    theta = 2.0 * math.pi * (np.arange(NQ) + 0.5) / NQ
    return [[(RADIUS / NQ * math.cos(k * theta[a]), RADIUS / NQ * math.sin(k * theta[a])) for a in range(4)] for k in range(1, 2 * MOM + 1)]


WEIGHTS = weights()


def split(value):
    high = value.astype(jnp.bfloat16)
    low = (value - high.astype(jnp.float32)).astype(jnp.bfloat16)
    return high, low


def dot3(lhs_high, lhs_low, rhs_high, rhs_low):
    dot = functools.partial(lax.dot_general, dimension_numbers=NT, preferred_element_type=jnp.float32)
    return dot(lhs_high, rhs_high) + dot(lhs_low, rhs_high) + dot(lhs_high, rhs_low)


def sweep_kernel(
    doms, probes, mass, blocks, coup, table, mom_ref, proj_ref,
    zb, yb, zk, yk, pz, py, pe_own, pe_in, pack, inv_re, inv_im, src, cw, rhi, rlo,
    y1r, y1i, y2r, y2i, y3r, y3i, gram,
    zs_send, zs_recv, ys_send, ys_recv, sz_send, sz_recv, sy_send, sy_recv, ps_send, ps_recv, es_send, es_recv,
):
    q = lax.axis_index("quad")
    d = lax.axis_index("dom")
    c = lax.rem(q, 2)
    o = 1 - c
    zl = lax.div(q, 2)
    zh = lax.rem(d, 2)
    flip = d + 1 - 2 * zh
    up = lax.rem(d + 2, doms)
    down = lax.rem(d + doms - 2, doms)
    y_to = lax.rem(d + 2 - 4 * zh + doms, doms)
    at_top = lax.div(q + 2, 8)
    at_bottom = 1 - lax.div(q + 6, 8)
    head = (1 - c) * at_top + c * at_bottom
    tail = (1 - c) * at_bottom + c * at_top
    q_to = lax.rem(q + 8 + 2 - 4 * c, 8)
    q_from = lax.rem(q + 8 - 2 + 4 * c, 8)
    d_to = d + head * (1 - 2 * zh)
    d_from = d + tail * (1 - 2 * zh)
    sib = q + 1 - 2 * c
    mirror = 2 * (3 - zl) + c
    is_head = head == 1

    barrier = pltpu.get_barrier_semaphore()

    def greet(quad, dom):
        pl.semaphore_signal(barrier, inc=1, device_id={"quad": quad, "dom": dom}, device_id_type=pl.DeviceIdType.MESH)

    greet(q_from, d_from)
    greet(sib, d)
    greet(mirror, flip)
    greet(q, up)
    greet(q, down)

    def copy(source, target, send, recv, quad, dom):
        return pltpu.make_async_remote_copy(
            src_ref=source, dst_ref=target, send_sem=send, recv_sem=recv,
            device_id={"quad": quad, "dom": dom}, device_id_type=pl.DeviceIdType.MESH,
        )

    def z_copy(s):
        if s == 0:
            return copy(zk.at[c], zk.at[c], zs_send.at[0], zs_recv.at[0], q_to, d_to)
        t = ORDER[s - 1]
        return copy(zb.at[c, t], zb.at[c, t], zs_send.at[s], zs_recv.at[s], q_to, d_to)

    def z_head(s):
        if s == 0:
            return copy(pack.at[c], zk.at[c], zs_send.at[0], zs_recv.at[0], q_to, d_to)
        t = ORDER[s - 1]
        line = zh * t + (1 - zh) * (LINES - 1 - t)
        return copy(blocks.at[c, line], zb.at[c, t], zs_send.at[s], zs_recv.at[s], q_to, d_to)

    def y_pack():
        return copy(zk.at[c], yk.at[c], ys_send.at[RIM], ys_recv.at[RIM], q, y_to)

    def y_copy(u):
        return copy(zb.at[c, LINES - 1 - u], yb.at[c, u], ys_send.at[u], ys_recv.at[u], q, y_to)

    def sz_pack(part):
        return copy(zk.at[part], zk.at[part], sz_send.at[RIM], sz_recv.at[RIM], sib, d)

    def sz_copy(t, part):
        return copy(zb.at[part, t], zb.at[part, t], sz_send.at[t], sz_recv.at[t], sib, d)

    def sy_pack(part):
        return copy(yk.at[part], yk.at[part], sy_send.at[RIM], sy_recv.at[RIM], sib, d)

    def sy_copy(u, part):
        return copy(yb.at[part, u], yb.at[part, u], sy_send.at[u], sy_recv.at[u], sib, d)

    p_mirror = copy(probes.at[:, pl.ds(mirror * OWNED * LINES, OWNED * LINES), :], pz, ps_send.at[0], ps_recv.at[0], mirror, flip)
    p_next = copy(pz, py, ps_send.at[1], ps_recv.at[1], q, y_to)
    e_up = copy(pe_own.at[1], pe_in.at[1], es_send.at[1], es_recv.at[1], q, up)
    e_down = copy(pe_own.at[0], pe_in.at[0], es_send.at[0], es_recv.at[0], q, down)

    eye = lax.broadcasted_iota(jnp.int32, (NY, NY), 0) == lax.broadcasted_iota(jnp.int32, (NY, NY), 1)

    for part in range(2):
        pack[part, 0:48, :] = coup[part]
        pack[part, 56:64, :] = mass[...]

    @pl.loop(0, LINES)
    def _(line):
        for part in range(2):
            diagonal = jnp.sum(jnp.where(eye, blocks[part, line], 0.0), axis=0, keepdims=True)
            pack[part, pl.ds(48 + line, 1), :] = diagonal

    for side, line in ((0, 0), (1, LINES - 1)):
        for part in range(2):
            pe_own[side, 8 * part : 8 * part + 8, :] = probes[part, pl.ds(q * OWNED * LINES + line, OWNED, stride=LINES), :]
            pe_own[side, 17 + part : 18 + part, :] = pack[part, 48 + line : 49 + line, :]
        pe_own[side, 16:17, :] = mass[line : line + 1, :]

    pl.semaphore_wait(barrier, 5)

    p_mirror.start()

    @pl.when(is_head)
    def _():
        for s in range(len(ORDER) + 1):
            z_head(s).start()

    e_up.start()
    e_down.start()

    def prepare(w, probe_re, probe_im, weight, diag_re, diag_im):
        line = d * LINES + zh * (w - FIRST) + (1 - zh) * (SPAN - 1 - FIRST - w)
        inside = jnp.logical_and(line >= 0, line < doms * LINES)
        source_re = weight * probe_re
        source_im = weight * probe_im
        src[w, 0] = source_re
        src[w, 1] = source_im
        denom_re = table[0] * weight - diag_re
        denom_im = table[1] * weight - diag_im
        modulus = denom_re * denom_re + denom_im * denom_im
        inv_re[w] = jnp.where(inside, denom_re / modulus, 0.0)
        inv_im[w] = jnp.where(inside, -denom_im / modulus, 0.0)
        for j in range(NQ):
            g_re = inv_re[w, j : j + 1, :]
            g_im = inv_im[w, j : j + 1, :]
            y1r[w, 8 * j : 8 * j + 8, :] = source_re * g_re - source_im * g_im
            y1i[w, 8 * j : 8 * j + 8, :] = source_re * g_im + source_im * g_re

    def couple(w, ref, line):
        for position in range(6):
            row = zh * position + (1 - zh) * (5 - position)
            for part in range(2):
                cw[w, 6 * part + position : 6 * part + position + 1, :] = ref[part, pl.ds(row * LINES + line, 1), :]

    def prepare_packed(w, line, probe, packed):
        couple(w, packed, line)
        prepare(
            w,
            probe[0, pl.ds(line, OWNED, stride=LINES), :],
            probe[1, pl.ds(line, OWNED, stride=LINES), :],
            packed[0, pl.ds(56 + line, 1), :],
            packed[0, pl.ds(48 + line, 1), :],
            packed[1, pl.ds(48 + line, 1), :],
        )

    def prepare_edge(w, side):
        prepare(w, pe_in[side, 0:8, :], pe_in[side, 8:16, :], pe_in[side, 16:17, :], pe_in[side, 17:18, :], pe_in[side, 18:19, :])

    def own_line(w):
        return zh * (w - FIRST) + (1 - zh) * (SPAN - 1 - FIRST - w)

    def operand(w, block_re, block_im):
        re_high, re_low = split(jnp.where(eye, 0.0, block_re))
        im_high, im_low = split(jnp.where(eye, 0.0, block_im))
        for ref, re, im in ((rhi, re_high, im_high), (rlo, re_low, im_low)):
            ref[w - 3, 0:NY, 0:NY] = re
            ref[w - 3, 0:NY, NY:] = -im
            ref[w - 3, NY:, 0:NY] = im
            ref[w - 3, NY:, NY:] = re

    def sweep(yr, yi, w, emit, order=range(NQ)):
        high, low = split(jnp.concatenate([yr[w], yi[w]], axis=1))
        image = dot3(high, low, rhi[w - 3], rlo[w - 3])
        c_re = [cw[w, i : i + 1, :] for i in range(6)]
        c_im = [cw[w, 6 + i : 7 + i, :] for i in range(6)]
        source_re = src[w, 0]
        source_im = src[w, 1]
        for j in order:
            rows = slice(8 * j, 8 * j + 8)
            a_re = image[rows, :NY] + source_re
            a_im = image[rows, NY:] + source_im
            for i, offset in enumerate(OFFSETS):
                n_re = yr[w + offset, rows, :]
                n_im = yi[w + offset, rows, :]
                a_re = a_re + (c_re[i] * n_re - c_im[i] * n_im)
                a_im = a_im + (c_re[i] * n_im + c_im[i] * n_re)
            g_re = inv_re[w, j : j + 1, :]
            g_im = inv_im[w, j : j + 1, :]
            emit(j, g_re * a_re - g_im * a_im, g_re * a_im + g_im * a_re)

    def second(w):
        def emit(j, re, im):
            y2r[w, 8 * j : 8 * j + 8, :] = re
            y2i[w, 8 * j : 8 * j + 8, :] = im

        sweep(y1r, y1i, w, emit)

    def third(w):
        def emit(j, re, im):
            y3r[w, 8 * j : 8 * j + 8, :] = re
            y3i[w, 8 * j : 8 * j + 8, :] = im

        sweep(y2r, y2i, w, emit)

    def last(w):
        line = own_line(w)
        field = {}

        def emit(j, re, im):
            field[j] = (re, im)

        sweep(y3r, y3i, w, emit, [a + 4 * b for a in range(4) for b in range(4)])
        sum_re = [None] * (2 * MOM)
        sum_im = [None] * (2 * MOM)
        for a in range(4):
            (r0, i0), (r1, i1), (r2, i2), (r3, i3) = (field[a + 4 * b] for b in range(4))
            er, ei, fr, fi = r0 + r2, i0 + i2, r0 - r2, i0 - i2
            gr, gi, hr, hi = r1 + r3, i1 + i3, r1 - r3, i1 - i3
            groups = ((er + gr, ei + gi), (fr - hi, fi + hr), (er - gr, ei - gi), (fr + hi, fi - hr))
            for k in range(2 * MOM):
                x_re, x_im = groups[(k + 1) % 4]
                w_re, w_im = WEIGHTS[k][a]
                t_re = w_re * x_re - w_im * x_im
                t_im = w_re * x_im + w_im * x_re
                sum_re[k] = t_re if a == 0 else sum_re[k] + t_re
                sum_im[k] = t_im if a == 0 else sum_im[k] + t_im
        for k in range(MOM):
            mom_ref[pl.ds(k * 16 + line, OWNED, stride=64), :] = sum_re[k]
            mom_ref[pl.ds(k * 16 + 8 + line, OWNED, stride=64), :] = sum_im[k]
        m_high, m_low = split(jnp.concatenate(sum_re + sum_im, axis=0))
        v_high, v_low = split(jnp.concatenate([probes[part, pl.ds(line, 64, stride=LINES), :] for part in range(2)], axis=0))
        gram[...] += dot3(v_high, v_low, m_high, m_low)

    def relay(s):
        z_copy(s).wait_recv()
        if s == 0:
            y_pack().start()
        elif ORDER[s - 1] >= 2:
            y_copy(LINES - 1 - ORDER[s - 1]).start()

        @pl.when(head == 0)
        def _():
            z_copy(s).start()

        if s == 0:
            sz_pack(c).start()
        elif ORDER[s - 1] < RIM:
            sz_copy(ORDER[s - 1], c).start()

    gram[...] = jnp.zeros_like(gram)

    @pl.loop(FIRST, FIRST + LINES)
    def _(w):
        line = own_line(w)
        couple(w, coup, line)
        prepare(
            w,
            probes[0, pl.ds(q * OWNED * LINES + line, OWNED, stride=LINES), :],
            probes[1, pl.ds(q * OWNED * LINES + line, OWNED, stride=LINES), :],
            mass[pl.ds(line, 1), :],
            pack[0, pl.ds(48 + line, 1), :],
            pack[1, pl.ds(48 + line, 1), :],
        )

    p_mirror.wait_recv()
    p_next.start()
    relay(0)
    relay(1)
    relay(2)

    @pl.loop(FIRST, FIRST + LINES)
    def _(w):
        line = own_line(w)
        operand(w, blocks[0, line], blocks[1, line])

    relay(3)
    sz_pack(o).wait_recv()
    e_down.wait_recv()
    e_up.wait_recv()

    @pl.loop(0, LINES)
    def _(t):
        prepare_packed(FIRST - 1 - t, (1 - zh) * t + zh * (LINES - 1 - t), pz, zk)

    prepare_edge(0, zh)
    relay(4)
    pl.loop(FIRST, FIRST + 2)(second)
    relay(5)
    pl.loop(FIRST + 2, FIRST + 4)(second)
    relay(6)
    pl.loop(FIRST + 4, FIRST + 5)(second)
    relay(7)
    relay(8)
    y_pack().wait_recv()
    sy_pack(c).start()
    for t in range(RIM):
        sz_copy(t, o).wait_recv()

    @pl.loop(0, RIM)
    def _(t):
        w = FIRST - 1 - t
        operand(w, zb[0, t], zb[1, t])
        second(w)

    p_next.wait_recv()
    sy_pack(o).wait_recv()

    @pl.loop(0, LINES)
    def _(u):
        prepare_packed(FIRST + LINES + u, (1 - zh) * (LINES - 1 - u) + zh * u, py, yk)

    prepare_edge(SPAN - 1, 1 - zh)
    y_copy(0).wait_recv()
    sy_copy(0, c).start()
    pl.loop(FIRST + 5, FIRST + 8)(second)
    pl.loop(FIRST - 3, FIRST + 5)(third)
    pl.loop(FIRST, FIRST + 2)(last)

    @pl.loop(0, RIM)
    def _(u):
        @pl.when(u < RIM - 1)
        def _():
            y_copy(u + 1).wait_recv()
            sy_copy(u + 1, c).start()

        sy_copy(u, o).wait_recv()
        w = FIRST + LINES + u
        operand(w, yb[0, u], yb[1, u])
        second(w)
        third(w - 3)
        last(w - 6)

    lane = lax.broadcasted_iota(jnp.int32, (64, 128), 1)
    other = pltpu.roll(gram[64:, :], 64, 1)
    scale = 1.0 / float(doms * LINES * NY)
    proj_ref[...] = scale * (gram[:64, :] + jnp.where(lane < 64, other, -other))

    p_mirror.wait_send()
    p_next.wait_send()
    e_up.wait_send()
    e_down.wait_send()
    for s in range(len(ORDER) + 1):
        z_copy(s).wait_send()
    y_pack().wait_send()
    sz_pack(c).wait_send()
    sy_pack(c).wait_send()
    for i in range(RIM):
        y_copy(i).wait_send()
        sz_copy(i, c).wait_send()
        sy_copy(i, c).wait_send()


def reduce_kernel(planes, part_ref, out_ref, mine, gathered, column, total, full, s1, r1, s2, r2, s3, r3):
    q = lax.axis_index("quad")
    d = lax.axis_index("dom")
    zh = lax.rem(d, 2)
    m = lax.div(d, 2)
    slot = zh * 8 + q
    rows = 64 // planes

    def dev(quad, dom):
        return {"quad": quad, "dom": dom}

    barrier = pltpu.get_barrier_semaphore()

    @pl.loop(1, planes)
    def _(i):
        pl.semaphore_signal(barrier, inc=1, device_id=dev(q, lax.rem(m + i, planes) * 2 + zh), device_id_type=pl.DeviceIdType.MESH)

    @pl.loop(1, 16)
    def _(i):
        to = lax.rem(slot + i, 16)
        pl.semaphore_signal(barrier, inc=1, device_id=dev(lax.rem(to, 8), 2 * m + lax.div(to, 8)), device_id_type=pl.DeviceIdType.MESH)

    for i in range(planes):
        mine[i] = part_ref[i * rows : (i + 1) * rows, :]
    pl.semaphore_wait(barrier, planes - 1 + 15)

    def plane_copy(i):
        to = lax.rem(m + i, planes)
        return pltpu.make_async_remote_copy(
            src_ref=mine.at[to], dst_ref=gathered.at[i], send_sem=s1.at[i], recv_sem=r1.at[i],
            device_id=dev(q, to * 2 + zh), device_id_type=pl.DeviceIdType.MESH,
        )

    def column_copy(i):
        to = lax.rem(slot + i, 16)
        return pltpu.make_async_remote_copy(
            src_ref=column.at[slot], dst_ref=column.at[slot], send_sem=s2.at[i], recv_sem=r2.at[i],
            device_id=dev(lax.rem(to, 8), 2 * m + lax.div(to, 8)), device_id_type=pl.DeviceIdType.MESH,
        )

    def column_arrived(i):
        come = lax.rem(slot + 16 - i, 16)
        return pltpu.make_async_remote_copy(
            src_ref=column.at[come], dst_ref=column.at[come], send_sem=s2.at[i], recv_sem=r2.at[i],
            device_id=dev(lax.rem(come, 8), 2 * m + lax.div(come, 8)), device_id_type=pl.DeviceIdType.MESH,
        )

    def full_copy(i):
        to = lax.rem(m + i, planes)
        return pltpu.make_async_remote_copy(
            src_ref=total, dst_ref=full.at[m], send_sem=s3.at[i], recv_sem=r3.at[i],
            device_id=dev(q, to * 2 + zh), device_id_type=pl.DeviceIdType.MESH,
        )

    def full_arrived(i):
        come = lax.rem(m + planes - i, planes)
        return pltpu.make_async_remote_copy(
            src_ref=total, dst_ref=full.at[come], send_sem=s3.at[i], recv_sem=r3.at[i],
            device_id=dev(q, come * 2 + zh), device_id_type=pl.DeviceIdType.MESH,
        )

    @pl.loop(1, planes)
    def _(i):
        plane_copy(i).start()

    gathered[0] = mine[m]

    @pl.loop(1, planes)
    def _(i):
        plane_copy(i).wait_recv()

    column[slot] = functools.reduce(lambda a, b: a + b, [gathered[i] for i in range(planes)])

    @pl.loop(1, 16)
    def _(i):
        column_copy(i).start()

    @pl.loop(1, 16)
    def _(i):
        column_arrived(i).wait_recv()

    for i in range(8):
        total[i] = column[i] + column[8 + i]

    @pl.loop(1, planes)
    def _(i):
        full_copy(i).start()

    full[m] = total[...]

    @pl.loop(1, planes)
    def _(i):
        full_arrived(i).wait_recv()

    out_ref[...] = full[...]

    @pl.loop(1, planes)
    def _(i):
        plane_copy(i).wait_send()
        full_copy(i).wait_send()

    @pl.loop(1, 16)
    def _(i):
        column_copy(i).wait_send()


def on_device(doms, probes, mass_weights, blocks, couplings):
    f32 = jnp.float32
    theta = 2.0 * math.pi * (np.arange(NQ) + 0.5) / NQ
    table = jnp.asarray(np.broadcast_to(np.stack([RADIUS * np.cos(theta), RADIUS * np.sin(theta)])[:, :, None], (2, NQ, NY)), f32)
    vmem = pl.BlockSpec(memory_space=pltpu.VMEM)
    dma = pltpu.SemaphoreType.DMA
    moments, partial = pl.pallas_call(
        functools.partial(sweep_kernel, doms),
        out_shape=(jax.ShapeDtypeStruct((512, NY), f32), jax.ShapeDtypeStruct((64, NY), f32)),
        in_specs=[vmem] * 5,
        out_specs=(vmem, vmem),
        scratch_shapes=[
            pltpu.VMEM((2, LINES, NY, NY), f32),
            pltpu.VMEM((2, RIM, NY, NY), f32),
            pltpu.VMEM((2, 64, NY), f32),
            pltpu.VMEM((2, 64, NY), f32),
            pltpu.VMEM((2, 64, NY), f32),
            pltpu.VMEM((2, 64, NY), f32),
            pltpu.VMEM((2, 24, NY), f32),
            pltpu.VMEM((2, 24, NY), f32),
            pltpu.VMEM((2, 64, NY), f32),
            pltpu.VMEM((SPAN, NQ, NY), f32),
            pltpu.VMEM((SPAN, NQ, NY), f32),
            pltpu.VMEM((SPAN, 2, OWNED, NY), f32),
            pltpu.VMEM((SPAN, 16, NY), f32),
            pltpu.VMEM((20, 2 * NY, 2 * NY), jnp.bfloat16),
            pltpu.VMEM((20, 2 * NY, 2 * NY), jnp.bfloat16),
        ]
        + [pltpu.VMEM((SPAN, NQ * OWNED, NY), f32)] * 6
        + [pltpu.VMEM((NY, NY), f32)]
        + [dma((9,)), dma((9,)), dma((7,)), dma((7,)), dma((7,)), dma((7,)), dma((7,)), dma((7,)), dma((2,)), dma((2,)), dma((2,)), dma((2,))],
        compiler_params=pltpu.CompilerParams(collective_id=0, has_side_effects=True, vmem_limit_bytes=48 * 1024 * 1024),
    )(
        probes.reshape(2, 512, NY),
        mass_weights,
        blocks,
        couplings.reshape(2, 48, NY),
        table,
    )
    planes = doms // 2
    rows = 64 // planes
    full = pl.pallas_call(
        functools.partial(reduce_kernel, planes),
        out_shape=jax.ShapeDtypeStruct((planes, 8, rows, NY), f32),
        in_specs=[vmem],
        out_specs=vmem,
        scratch_shapes=[
            pltpu.VMEM((planes, rows, NY), f32),
            pltpu.VMEM((planes, rows, NY), f32),
            pltpu.VMEM((16, rows, NY), f32),
            pltpu.VMEM((8, rows, NY), f32),
            pltpu.VMEM((planes, 8, rows, NY), f32),
        ]
        + [dma((16,))] * 6,
        compiler_params=pltpu.CompilerParams(collective_id=1, has_side_effects=True),
    )(partial)
    projected = full.reshape(planes, 8, rows, 2, 8, 8).transpose(3, 4, 0, 2, 1, 5).reshape(2, 8, 64, 64)
    return moments.reshape(OWNED, MOM, 2, LINES, NY), projected


def solution(mesh):
    return jax.shard_map(
        functools.partial(on_device, mesh.shape["dom"]),
        mesh=mesh,
        in_specs=(P(None, None, "dom", None), P("dom", None), P(None, "dom", None, None), P(None, None, "dom", None)),
        out_specs=(P("quad", None, None, "dom", None), P()),
        check_vma=False,
    )
```

```python
import functools
import math

import jax
import jax.numpy as jnp
import numpy as np
from jax import lax
from jax.experimental import pallas as pl
from jax.experimental.pallas import tpu as pltpu
from jax.sharding import PartitionSpec as P

NQ = 16
MOM = 4
RADIUS = 2.0
OFFSETS = (-3, -2, -1, 1, 2, 3)
LINES = 8
OWNED = 8
NY = 128
FIRST = 9
SPAN = 26
ORDER = (7, 0, 6, 1, 5, 4, 3, 2)
RIM = 6
NT = (((1,), (1,)), ((), ()))


def weights():
    theta = 2.0 * math.pi * (np.arange(NQ) + 0.5) / NQ
    return [[(RADIUS / NQ * math.cos(k * theta[a]), RADIUS / NQ * math.sin(k * theta[a])) for a in range(4)] for k in range(1, 2 * MOM + 1)]


WEIGHTS = weights()


def split(value):
    high = value.astype(jnp.bfloat16)
    low = (value - high.astype(jnp.float32)).astype(jnp.bfloat16)
    return high, low


def dot3(lhs, rhs_high, rhs_low):
    dot = functools.partial(lax.dot_general, dimension_numbers=NT, preferred_element_type=jnp.float32)
    high, low = split(lhs)
    count = lhs.shape[0]
    both = dot(jnp.concatenate([high, low], axis=0), rhs_high)
    return both[:count] + both[count:] + dot(high, rhs_low)


def sweep_kernel(
    doms, probes_hbm, mass_hbm, blocks_hbm, coup_hbm, mom_ref, out_ref,
    probes, blocks, table, zb, yb, zk, yk, pz, py, pe_own, pe_in, pack, inv_re, inv_im, src, cw, rhi, rlo,
    y1r, y1i, y2r, y2i, y3r, y3i, ima, imb, imc, gram, mine, gathered, column, total, full,
    in_sem, zs_send, zs_recv, ys_send, ys_recv, sz_send, sz_recv, sy_send, sy_recv, ps_send, ps_recv, es_send, es_recv,
    s1, r1, s2, r2, s3, r3,
):
    q = lax.axis_index("quad")
    d = lax.axis_index("dom")
    c = lax.rem(q, 2)
    o = 1 - c
    zl = lax.div(q, 2)
    zh = lax.rem(d, 2)
    flip = d + 1 - 2 * zh
    up = lax.rem(d + 2, doms)
    down = lax.rem(d + doms - 2, doms)
    y_to = lax.rem(d + 2 - 4 * zh + doms, doms)
    at_top = lax.div(q + 2, 8)
    at_bottom = 1 - lax.div(q + 6, 8)
    head = (1 - c) * at_top + c * at_bottom
    tail = (1 - c) * at_bottom + c * at_top
    q_to = lax.rem(q + 8 + 2 - 4 * c, 8)
    q_from = lax.rem(q + 8 - 2 + 4 * c, 8)
    d_to = d + head * (1 - 2 * zh)
    d_from = d + tail * (1 - 2 * zh)
    sib = q + 1 - 2 * c
    mirror = 2 * (3 - zl) + c
    is_head = head == 1
    far = lax.div(c * (3 - zl) + (1 - c) * zl, 2) == 1
    planes = doms // 2
    rows = 64 // planes
    m = lax.div(d, 2)
    slot = zh * 8 + q

    arrivals = [
        pltpu.make_async_copy(coup_hbm, pack.at[:, pl.ds(0, 48), :], in_sem.at[0]),
        pltpu.make_async_copy(mass_hbm, pack.at[0, pl.ds(56, 8), :], in_sem.at[1]),
        pltpu.make_async_copy(mass_hbm, pack.at[1, pl.ds(56, 8), :], in_sem.at[2]),
        pltpu.make_async_copy(probes_hbm, probes, in_sem.at[3]),
        pltpu.make_async_copy(blocks_hbm, blocks, in_sem.at[4]),
    ]
    for arrival in arrivals:
        arrival.start()

    barrier = pltpu.get_barrier_semaphore()

    def greet(quad, dom):
        pl.semaphore_signal(barrier, inc=1, device_id={"quad": quad, "dom": dom}, device_id_type=pl.DeviceIdType.MESH)

    greet(mirror, flip)
    greet(q_from, d_from)
    greet(q, up)
    greet(q, down)
    greet(sib, d)

    @pl.loop(1, planes)
    def _(i):
        greet(q, lax.rem(m + i, planes) * 2 + zh)

    @pl.loop(1, 16)
    def _(i):
        to = lax.rem(slot + i, 16)
        greet(lax.rem(to, 8), 2 * m + lax.div(to, 8))

    def copy(source, target, send, recv, quad, dom):
        return pltpu.make_async_remote_copy(
            src_ref=source, dst_ref=target, send_sem=send, recv_sem=recv,
            device_id={"quad": quad, "dom": dom}, device_id_type=pl.DeviceIdType.MESH,
        )

    def z_copy(s):
        t = ORDER[s]
        return copy(zb.at[c, t], zb.at[c, t], zs_send.at[s], zs_recv.at[s], q_to, d_to)

    def z_head(s):
        t = ORDER[s]
        line = zh * t + (1 - zh) * (LINES - 1 - t)
        return copy(blocks_hbm.at[c, line], zb.at[c, t], zs_send.at[s], zs_recv.at[s], q_to, d_to)

    def y_pack():
        return copy(zk.at[c], yk.at[c], ys_send.at[RIM], ys_recv.at[RIM], q, y_to)

    def y_copy(u):
        return copy(zb.at[c, LINES - 1 - u], yb.at[c, u], ys_send.at[u], ys_recv.at[u], q, y_to)

    def sz_pack(part):
        return copy(zk.at[part], zk.at[part], sz_send.at[RIM], sz_recv.at[RIM], sib, d)

    def sz_copy(t, part):
        return copy(zb.at[part, t], zb.at[part, t], sz_send.at[t], sz_recv.at[t], sib, d)

    def sy_pack(part):
        return copy(yk.at[part], yk.at[part], sy_send.at[RIM], sy_recv.at[RIM], sib, d)

    def sy_copy(u, part):
        return copy(yb.at[part, u], yb.at[part, u], sy_send.at[u], sy_recv.at[u], sib, d)

    k_mirror = copy(pack.at[c], zk.at[c], ps_send.at[2], ps_recv.at[2], mirror, flip)
    p_mirror = copy(probes_hbm.at[:, pl.ds(mirror * OWNED * LINES, OWNED * LINES), :], pz, ps_send.at[0], ps_recv.at[0], mirror, flip)
    p_next = copy(pz, py, ps_send.at[1], ps_recv.at[1], q, y_to)
    e_up = copy(pe_own.at[1], pe_in.at[1], es_send.at[1], es_recv.at[1], q, up)
    e_down = copy(pe_own.at[0], pe_in.at[0], es_send.at[0], es_recv.at[0], q, down)

    eye = lax.broadcasted_iota(jnp.int32, (NY, NY), 0) == lax.broadcasted_iota(jnp.int32, (NY, NY), 1)

    row = lax.broadcasted_iota(jnp.int32, (NQ, NY), 0)
    for part, function in ((0, math.cos), (1, math.sin)):
        values = jnp.zeros((NQ, NY), jnp.float32)
        for j in range(NQ):
            values = jnp.where(row == j, RADIUS * function(2.0 * math.pi * (j + 0.5) / NQ), values)
        table[part] = values
    for arrival in arrivals:
        arrival.wait()

    @pl.loop(0, LINES)
    def _(line):
        for part in range(2):
            diagonal = jnp.sum(jnp.where(eye, blocks[part, line], 0.0), axis=0, keepdims=True)
            pack[part, pl.ds(48 + line, 1), :] = diagonal

    for side, line in ((0, 0), (1, LINES - 1)):
        for part in range(2):
            pe_own[side, 8 * part : 8 * part + 8, :] = probes[part, pl.ds(q * OWNED * LINES + line, OWNED, stride=LINES), :]
            pe_own[side, 17 + part : 18 + part, :] = pack[part, 48 + line : 49 + line, :]
        pe_own[side, 16:17, :] = pack[0, 56 + line : 57 + line, :]

    pl.semaphore_wait(barrier, 5 + planes - 1 + 15)

    @pl.when(is_head)
    def _():
        for s in range(len(ORDER)):
            z_head(s).start()

    k_mirror.start()
    p_mirror.start()
    e_up.start()
    e_down.start()

    def prepare(w, probe_re, probe_im, weight, diag_re, diag_im):
        line = d * LINES + zh * (w - FIRST) + (1 - zh) * (SPAN - 1 - FIRST - w)
        inside = jnp.logical_and(line >= 0, line < doms * LINES)
        source_re = weight * probe_re
        source_im = weight * probe_im
        src[w, 0] = source_re
        src[w, 1] = source_im
        denom_re = table[0] * weight - diag_re
        denom_im = table[1] * weight - diag_im
        modulus = denom_re * denom_re + denom_im * denom_im
        inv_re[w] = jnp.where(inside, denom_re / modulus, 0.0)
        inv_im[w] = jnp.where(inside, -denom_im / modulus, 0.0)
        for j in range(NQ):
            g_re = inv_re[w, j : j + 1, :]
            g_im = inv_im[w, j : j + 1, :]
            y1r[w, 8 * j : 8 * j + 8, :] = source_re * g_re - source_im * g_im
            y1i[w, 8 * j : 8 * j + 8, :] = source_re * g_im + source_im * g_re

    def couple(w, ref, line):
        for position in range(6):
            row = zh * position + (1 - zh) * (5 - position)
            for part in range(2):
                cw[w, 6 * part + position : 6 * part + position + 1, :] = ref[part, pl.ds(row * LINES + line, 1), :]

    def prepare_packed(w, line, probe, packed):
        couple(w, packed, line)
        prepare(
            w,
            probe[0, pl.ds(line, OWNED, stride=LINES), :],
            probe[1, pl.ds(line, OWNED, stride=LINES), :],
            packed[0, pl.ds(56 + line, 1), :],
            packed[0, pl.ds(48 + line, 1), :],
            packed[1, pl.ds(48 + line, 1), :],
        )

    def prepare_edge(w, side):
        prepare(w, pe_in[side, 0:8, :], pe_in[side, 8:16, :], pe_in[side, 16:17, :], pe_in[side, 17:18, :], pe_in[side, 18:19, :])

    def own_line(w):
        return zh * (w - FIRST) + (1 - zh) * (SPAN - 1 - FIRST - w)

    def operand(w, block_re, block_im):
        re_high, re_low = split(jnp.where(eye, 0.0, block_re))
        im_high, im_low = split(jnp.where(eye, 0.0, block_im))
        for ref, re, im in ((rhi, re_high, im_high), (rlo, re_low, im_low)):
            ref[w - 3, 0:NY, 0:NY] = re
            ref[w - 3, 0:NY, NY:] = -im
            ref[w - 3, NY:, 0:NY] = im
            ref[w - 3, NY:, NY:] = re

    def image(yr, yi, w, into):
        into[...] = dot3(jnp.concatenate([yr[w], yi[w]], axis=1), rhi[w - 3], rlo[w - 3])

    def finish(yr, yi, w, image_ref, emit, order=range(NQ)):
        c_re = [cw[w, i : i + 1, :] for i in range(6)]
        c_im = [cw[w, 6 + i : 7 + i, :] for i in range(6)]
        source_re = src[w, 0]
        source_im = src[w, 1]
        for j in order:
            part = slice(8 * j, 8 * j + 8)
            a_re = image_ref[part, :NY] + source_re
            a_im = image_ref[part, NY:] + source_im
            for i, offset in enumerate(OFFSETS):
                n_re = yr[w + offset, part, :]
                n_im = yi[w + offset, part, :]
                a_re = a_re + (c_re[i] * n_re - c_im[i] * n_im)
                a_im = a_im + (c_re[i] * n_im + c_im[i] * n_re)
            g_re = inv_re[w, j : j + 1, :]
            g_im = inv_im[w, j : j + 1, :]
            emit(j, g_re * a_re - g_im * a_im, g_re * a_im + g_im * a_re)

    def keep(yr, yi, w):
        def emit(j, re, im):
            yr[w, 8 * j : 8 * j + 8, :] = re
            yi[w, 8 * j : 8 * j + 8, :] = im

        return emit

    def second(w, image_ref):
        finish(y1r, y1i, w, image_ref, keep(y2r, y2i, w))

    def third(w, image_ref):
        finish(y2r, y2i, w, image_ref, keep(y3r, y3i, w))

    def last(w, image_ref):
        line = own_line(w)
        field = {}

        def emit(j, re, im):
            field[j] = (re, im)

        finish(y3r, y3i, w, image_ref, emit, [a + 4 * b for a in range(4) for b in range(4)])
        sum_re = [None] * (2 * MOM)
        sum_im = [None] * (2 * MOM)
        for a in range(4):
            (r0, i0), (r1, i1), (r2, i2), (r3, i3) = (field[a + 4 * b] for b in range(4))
            er, ei, fr, fi = r0 + r2, i0 + i2, r0 - r2, i0 - i2
            gr, gi, hr, hi = r1 + r3, i1 + i3, r1 - r3, i1 - i3
            groups = ((er + gr, ei + gi), (fr - hi, fi + hr), (er - gr, ei - gi), (fr + hi, fi - hr))
            for k in range(2 * MOM):
                x_re, x_im = groups[(k + 1) % 4]
                w_re, w_im = WEIGHTS[k][a]
                t_re = w_re * x_re - w_im * x_im
                t_im = w_re * x_im + w_im * x_re
                sum_re[k] = t_re if a == 0 else sum_re[k] + t_re
                sum_im[k] = t_im if a == 0 else sum_im[k] + t_im
        for k in range(MOM):
            mom_ref[pl.ds(k * 16 + line, OWNED, stride=64), :] = sum_re[k]
            mom_ref[pl.ds(k * 16 + 8 + line, OWNED, stride=64), :] = sum_im[k]
        m_high, m_low = split(jnp.concatenate(sum_re + sum_im, axis=0))
        probe_lines = jnp.concatenate([probes[part, pl.ds(line, 64, stride=LINES), :] for part in range(2)], axis=0)
        gram[...] += dot3(probe_lines, m_high, m_low)

    def pairs(yr, yi, step, first, count):
        image(yr, yi, first, ima)

        @pl.loop(0, count // 2)
        def _(i):
            w = first + 2 * i
            image(yr, yi, w + 1, imb)
            step(w, ima)
            image(yr, yi, jnp.minimum(w + 2, first + count - 1), ima)
            step(w + 1, imb)

    def relay(s):
        z_copy(s).wait_recv()
        if ORDER[s] >= 2:
            y_copy(LINES - 1 - ORDER[s]).start()

        @pl.when(head == 0)
        def _():
            z_copy(s).start()

        if ORDER[s] < RIM:
            sz_copy(ORDER[s], c).start()

    def pass_small():
        k_mirror.wait_recv()
        y_pack().start()
        sz_pack(c).start()
        p_mirror.wait_recv()
        p_next.start()

    def prepare_z():
        sz_pack(o).wait_recv()
        e_down.wait_recv()
        e_up.wait_recv()

        @pl.loop(0, LINES)
        def _(t):
            prepare_packed(FIRST - 1 - t, (1 - zh) * t + zh * (LINES - 1 - t), pz, zk)

        prepare_edge(0, zh)

    def prepare_y():
        y_pack().wait_recv()
        sy_pack(c).start()
        p_next.wait_recv()
        sy_pack(o).wait_recv()

        @pl.loop(0, LINES)
        def _(u):
            prepare_packed(FIRST + LINES + u, (1 - zh) * (LINES - 1 - u) + zh * u, py, yk)

        prepare_edge(SPAN - 1, 1 - zh)

    gram[...] = jnp.zeros_like(gram)

    @pl.loop(FIRST, FIRST + LINES)
    def _(w):
        line = own_line(w)
        couple(w, pack, line)
        prepare(
            w,
            probes[0, pl.ds(q * OWNED * LINES + line, OWNED, stride=LINES), :],
            probes[1, pl.ds(q * OWNED * LINES + line, OWNED, stride=LINES), :],
            pack[0, pl.ds(56 + line, 1), :],
            pack[0, pl.ds(48 + line, 1), :],
            pack[1, pl.ds(48 + line, 1), :],
        )
        operand(w, blocks[0, line], blocks[1, line])

    @pl.when(far)
    def _():
        pass_small()
        prepare_z()
        pairs(y1r, y1i, second, FIRST, 4)

    relay(0)
    relay(1)
    pl.when(jnp.logical_not(far))(pass_small)
    relay(2)
    pl.when(jnp.logical_not(far))(prepare_z)
    relay(3)

    @pl.when(far)
    def _():
        prepare_y()

    @pl.when(jnp.logical_not(far))
    def _():
        pairs(y1r, y1i, second, FIRST, 2)

    relay(4)

    @pl.when(far)
    def _():
        pairs(y1r, y1i, second, FIRST + 4, 2)

    @pl.when(jnp.logical_not(far))
    def _():
        pairs(y1r, y1i, second, FIRST + 2, 2)

    relay(5)

    @pl.when(far)
    def _():
        pairs(y1r, y1i, second, FIRST + 6, 2)

    relay(6)
    relay(7)

    @pl.when(jnp.logical_not(far))
    def _():
        prepare_y()
        pairs(y1r, y1i, second, FIRST + 4, 4)

    @pl.loop(0, 3)
    def _(i):
        t = lax.rem(4 * i, RIM)
        w = FIRST - 1 - t
        sz_copy(t, o).wait_recv()
        operand(w, zb[0, t], zb[1, t])
        image(y1r, y1i, w, ima)
        sz_copy(t + 1, o).wait_recv()
        operand(w - 1, zb[0, t + 1], zb[1, t + 1])
        image(y1r, y1i, w - 1, imb)
        second(w, ima)
        second(w - 1, imb)

    y_copy(0).wait_recv()
    sy_copy(0, c).start()
    pairs(y2r, y2i, third, FIRST - 3, 8)
    pairs(y3r, y3i, last, FIRST, 2)

    @pl.loop(0, RIM)
    def _(u):
        @pl.when(u < RIM - 1)
        def _():
            y_copy(u + 1).wait_recv()
            sy_copy(u + 1, c).start()

        sy_copy(u, o).wait_recv()
        w = FIRST + LINES + u
        image(y3r, y3i, w - 6, imc)
        image(y2r, y2i, w - 3, imb)
        operand(w, yb[0, u], yb[1, u])
        image(y1r, y1i, w, ima)
        second(w, ima)
        third(w - 3, imb)
        last(w - 6, imc)

    lane = lax.broadcasted_iota(jnp.int32, (64, 128), 1)
    other = pltpu.roll(gram[64:, :], 64, 1)
    scale = 1.0 / float(doms * LINES * NY)
    partial = scale * (gram[:64, :] + jnp.where(lane < 64, other, -other))
    for i in range(planes):
        mine[i] = partial[i * rows : (i + 1) * rows, :]

    def dev(quad, dom):
        return {"quad": quad, "dom": dom}

    def plane_copy(i):
        to = lax.rem(m + i, planes)
        return pltpu.make_async_remote_copy(
            src_ref=mine.at[to], dst_ref=gathered.at[i], send_sem=s1.at[i], recv_sem=r1.at[i],
            device_id=dev(q, to * 2 + zh), device_id_type=pl.DeviceIdType.MESH,
        )

    def column_copy(i):
        to = lax.rem(slot + i, 16)
        return pltpu.make_async_remote_copy(
            src_ref=column.at[slot], dst_ref=column.at[slot], send_sem=s2.at[i], recv_sem=r2.at[i],
            device_id=dev(lax.rem(to, 8), 2 * m + lax.div(to, 8)), device_id_type=pl.DeviceIdType.MESH,
        )

    def column_arrived(i):
        come = lax.rem(slot + 16 - i, 16)
        return pltpu.make_async_remote_copy(
            src_ref=column.at[come], dst_ref=column.at[come], send_sem=s2.at[i], recv_sem=r2.at[i],
            device_id=dev(lax.rem(come, 8), 2 * m + lax.div(come, 8)), device_id_type=pl.DeviceIdType.MESH,
        )

    def full_copy(i):
        to = lax.rem(m + i, planes)
        return pltpu.make_async_remote_copy(
            src_ref=total, dst_ref=full.at[m], send_sem=s3.at[i], recv_sem=r3.at[i],
            device_id=dev(q, to * 2 + zh), device_id_type=pl.DeviceIdType.MESH,
        )

    def full_arrived(i):
        come = lax.rem(m + planes - i, planes)
        return pltpu.make_async_remote_copy(
            src_ref=total, dst_ref=full.at[come], send_sem=s3.at[i], recv_sem=r3.at[i],
            device_id=dev(q, come * 2 + zh), device_id_type=pl.DeviceIdType.MESH,
        )

    @pl.loop(1, planes)
    def _(i):
        plane_copy(i).start()

    gathered[0] = mine[m]

    @pl.loop(1, planes)
    def _(i):
        plane_copy(i).wait_recv()

    column[slot] = functools.reduce(lambda a, b: a + b, [gathered[i] for i in range(planes)])

    @pl.loop(1, 16)
    def _(i):
        column_copy(i).start()

    @pl.loop(1, 16)
    def _(i):
        column_arrived(i).wait_recv()

    group = lax.div(lax.broadcasted_iota(jnp.int32, (rows, NY), 1), 8)
    sums = [column[i] + column[8 + i] for i in range(8)]
    for pair in range(8):
        value = jnp.zeros((rows, NY), jnp.float32)
        for half in range(2):
            for i in range(8):
                to = 8 * half + i
                shift = (to - 2 * pair - half) % 16 * 8
                moved = pltpu.roll(sums[i], shift, 1) if shift else sums[i]
                value = jnp.where(group == to, moved, value)
        total[pair] = value

    @pl.loop(1, planes)
    def _(i):
        full_copy(i).start()

    full[m] = total[...]

    @pl.loop(1, planes)
    def _(i):
        full_arrived(i).wait_recv()

    for i in range(planes):
        for pair in range(8):
            value = full[i, pair]
            out_ref[2 * pair, rows * i : rows * (i + 1), :] = value[:, :64]
            out_ref[2 * pair + 1, rows * i : rows * (i + 1), :] = value[:, 64:]

    @pl.loop(1, planes)
    def _(i):
        plane_copy(i).wait_send()
        full_copy(i).wait_send()

    @pl.loop(1, 16)
    def _(i):
        column_copy(i).wait_send()

    k_mirror.wait_send()
    p_mirror.wait_send()
    p_next.wait_send()
    e_up.wait_send()
    e_down.wait_send()
    for s in range(len(ORDER)):
        z_copy(s).wait_send()
    y_pack().wait_send()
    sz_pack(c).wait_send()
    sy_pack(c).wait_send()
    for i in range(RIM):
        y_copy(i).wait_send()
        sz_copy(i, c).wait_send()
        sy_copy(i, c).wait_send()


def on_device(doms, probes, mass_weights, blocks, couplings):
    f32 = jnp.float32
    planes = doms // 2
    rows = 64 // planes
    vmem = pl.BlockSpec(memory_space=pltpu.VMEM)
    dma = pltpu.SemaphoreType.DMA
    moments, projected = pl.pallas_call(
        functools.partial(sweep_kernel, doms),
        out_shape=(jax.ShapeDtypeStruct((512, NY), f32), jax.ShapeDtypeStruct((16, 64, 64), f32)),
        in_specs=[pl.BlockSpec(memory_space=pl.ANY)] * 4,
        out_specs=(vmem, vmem),
        scratch_shapes=[
            pltpu.VMEM((2, 512, NY), f32),
            pltpu.VMEM((2, LINES, NY, NY), f32),
            pltpu.VMEM((2, NQ, NY), f32),
            pltpu.VMEM((2, LINES, NY, NY), f32),
            pltpu.VMEM((2, RIM, NY, NY), f32),
            pltpu.VMEM((2, 64, NY), f32),
            pltpu.VMEM((2, 64, NY), f32),
            pltpu.VMEM((2, 64, NY), f32),
            pltpu.VMEM((2, 64, NY), f32),
            pltpu.VMEM((2, 24, NY), f32),
            pltpu.VMEM((2, 24, NY), f32),
            pltpu.VMEM((2, 64, NY), f32),
            pltpu.VMEM((SPAN, NQ, NY), f32),
            pltpu.VMEM((SPAN, NQ, NY), f32),
            pltpu.VMEM((SPAN, 2, OWNED, NY), f32),
            pltpu.VMEM((SPAN, 16, NY), f32),
            pltpu.VMEM((20, 2 * NY, 2 * NY), jnp.bfloat16),
            pltpu.VMEM((20, 2 * NY, 2 * NY), jnp.bfloat16),
        ]
        + [pltpu.VMEM((SPAN, NQ * OWNED, NY), f32)] * 6
        + [pltpu.VMEM((NY, 2 * NY), f32)] * 3
        + [
            pltpu.VMEM((NY, NY), f32),
            pltpu.VMEM((planes, rows, NY), f32),
            pltpu.VMEM((planes, rows, NY), f32),
            pltpu.VMEM((16, rows, NY), f32),
            pltpu.VMEM((8, rows, NY), f32),
            pltpu.VMEM((planes, 8, rows, NY), f32),
        ]
        + [dma((5,))]
        + [dma((8,))] * 2
        + [dma((7,))] * 6
        + [dma((3,))] * 2
        + [dma((2,))] * 2
        + [dma((16,))] * 6,
        compiler_params=pltpu.CompilerParams(collective_id=0, has_side_effects=True, vmem_limit_bytes=60 * 1024 * 1024),
    )(probes.reshape(2, 512, NY), mass_weights, blocks, couplings.reshape(2, 48, NY))
    return moments.reshape(OWNED, MOM, 2, LINES, NY), projected.reshape(2, 8, 64, 64)


def solution(mesh):
    return jax.shard_map(
        functools.partial(on_device, mesh.shape["dom"]),
        mesh=mesh,
        in_specs=(P(None, None, "dom", None), P("dom", None), P(None, "dom", None, None), P(None, None, "dom", None)),
        out_specs=(P("quad", None, None, "dom", None), P()),
        check_vma=False,
    )
```

```python
import functools
import math

import jax
import jax.numpy as jnp
import numpy as np
from jax import lax
from jax.experimental import pallas as pl
from jax.experimental.pallas import tpu as pltpu
from jax.sharding import PartitionSpec as P

NQ = 16
MOM = 4
RADIUS = 2.0
OFFSETS = (-3, -2, -1, 1, 2, 3)
LINES = 8
OWNED = 8
NY = 128
FIRST = 9
SPAN = 26
ORDER = (7, 0, 6, 1, 5, 4, 3, 2)
RIM = 6
PLANE_ORDER = (10, 6, 9, 11, 14, 2, 8, 5, 7, 13, 3, 15, 1, 12, 4)
COLUMN_ORDER = (8, 7, 9, 6, 10, 5, 11, 4, 12, 3, 13, 2, 14, 15, 1)
NT = (((1,), (1,)), ((), ()))


def weights():
    theta = 2.0 * math.pi * (np.arange(NQ) + 0.5) / NQ
    return [[(RADIUS / NQ * math.cos(k * theta[a]), RADIUS / NQ * math.sin(k * theta[a])) for a in range(4)] for k in range(1, 2 * MOM + 1)]


WEIGHTS = weights()


def split(value):
    high = value.astype(jnp.bfloat16)
    low = (value - high.astype(jnp.float32)).astype(jnp.bfloat16)
    return high, low


def dot3(lhs, rhs_high, rhs_low):
    dot = functools.partial(lax.dot_general, dimension_numbers=NT, preferred_element_type=jnp.float32)
    high, low = split(lhs)
    count = lhs.shape[0]
    both = dot(jnp.concatenate([high, low], axis=0), rhs_high)
    return both[:count] + both[count:] + dot(high, rhs_low)


def sweep_kernel(
    doms, probes_hbm, mass_hbm, blocks_hbm, coup_hbm, mom_ref, out_ref,
    probes, blocks, table, zb, yb, zk, yk, pz, py, pe_own, pe_in, pack, inv_re, inv_im, src, cw, rhi, rlo,
    y1r, y1i, y2r, y2i, y3r, y3i, ima, imb, imc, gram, mine, gathered, column, total, full,
    in_sem, zs_send, zs_recv, ys_send, ys_recv, sz_send, sz_recv, sy_send, sy_recv, ps_send, ps_recv, es_send, es_recv,
    s1, r1, s2, r2, s3, r3,
):
    q = lax.axis_index("quad")
    d = lax.axis_index("dom")
    c = lax.rem(q, 2)
    o = 1 - c
    zl = lax.div(q, 2)
    zh = lax.rem(d, 2)
    flip = d + 1 - 2 * zh
    up = lax.rem(d + 2, doms)
    down = lax.rem(d + doms - 2, doms)
    y_to = lax.rem(d + 2 - 4 * zh + doms, doms)
    at_top = lax.div(q + 2, 8)
    at_bottom = 1 - lax.div(q + 6, 8)
    head = (1 - c) * at_top + c * at_bottom
    tail = (1 - c) * at_bottom + c * at_top
    q_to = lax.rem(q + 8 + 2 - 4 * c, 8)
    q_from = lax.rem(q + 8 - 2 + 4 * c, 8)
    d_to = d + head * (1 - 2 * zh)
    d_from = d + tail * (1 - 2 * zh)
    sib = q + 1 - 2 * c
    mirror = 2 * (3 - zl) + c
    is_head = head == 1
    far = lax.div(c * (3 - zl) + (1 - c) * zl, 2) == 1
    planes = doms // 2
    rows = 64 // planes
    m = lax.div(d, 2)
    slot = zh * 8 + q

    arrivals = [
        pltpu.make_async_copy(coup_hbm, pack.at[:, pl.ds(0, 48), :], in_sem.at[0]),
        pltpu.make_async_copy(mass_hbm, pack.at[0, pl.ds(56, 8), :], in_sem.at[1]),
        pltpu.make_async_copy(mass_hbm, pack.at[1, pl.ds(56, 8), :], in_sem.at[2]),
        pltpu.make_async_copy(probes_hbm, probes, in_sem.at[3]),
        pltpu.make_async_copy(blocks_hbm, blocks, in_sem.at[4]),
    ]
    for arrival in arrivals:
        arrival.start()

    barrier = pltpu.get_barrier_semaphore()

    def greet(quad, dom):
        pl.semaphore_signal(barrier, inc=1, device_id={"quad": quad, "dom": dom}, device_id_type=pl.DeviceIdType.MESH)

    greet(mirror, flip)
    greet(q_from, d_from)
    greet(q, up)
    greet(q, down)
    greet(sib, d)

    @pl.loop(1, planes)
    def _(i):
        greet(q, lax.rem(m + i, planes) * 2 + zh)

    @pl.loop(1, 16)
    def _(i):
        to = lax.rem(slot + i, 16)
        greet(lax.rem(to, 8), 2 * m + lax.div(to, 8))

    def copy(source, target, send, recv, quad, dom):
        return pltpu.make_async_remote_copy(
            src_ref=source, dst_ref=target, send_sem=send, recv_sem=recv,
            device_id={"quad": quad, "dom": dom}, device_id_type=pl.DeviceIdType.MESH,
        )

    def z_copy(s):
        t = ORDER[s // 2]
        piece = zb.at[c, t, pl.ds(s % 2 * 64, 64), :]
        return copy(piece, piece, zs_send.at[s], zs_recv.at[s], q_to, d_to)

    def z_head(s):
        t = ORDER[s // 2]
        half = pl.ds(s % 2 * 64, 64)
        line = zh * t + (1 - zh) * (LINES - 1 - t)
        return copy(blocks_hbm.at[c, line, half, :], zb.at[c, t, half, :], zs_send.at[s], zs_recv.at[s], q_to, d_to)

    def y_pack():
        return copy(zk.at[c], yk.at[c], ys_send.at[RIM], ys_recv.at[RIM], q, y_to)

    def y_copy(u):
        return copy(zb.at[c, LINES - 1 - u], yb.at[c, u], ys_send.at[u], ys_recv.at[u], q, y_to)

    def sz_pack(part):
        return copy(zk.at[part], zk.at[part], sz_send.at[RIM], sz_recv.at[RIM], sib, d)

    def sz_copy(t, part):
        return copy(zb.at[part, t], zb.at[part, t], sz_send.at[t], sz_recv.at[t], sib, d)

    def sy_pack(part):
        return copy(yk.at[part], yk.at[part], sy_send.at[RIM], sy_recv.at[RIM], sib, d)

    def sy_copy(u, part):
        return copy(yb.at[part, u], yb.at[part, u], sy_send.at[u], sy_recv.at[u], sib, d)

    k_mirror = copy(pack.at[c], zk.at[c], ps_send.at[2], ps_recv.at[2], mirror, flip)
    p_mirror = copy(probes_hbm.at[:, pl.ds(mirror * OWNED * LINES, OWNED * LINES), :], pz, ps_send.at[0], ps_recv.at[0], mirror, flip)
    p_next = copy(pz, py, ps_send.at[1], ps_recv.at[1], q, y_to)
    e_up = copy(pe_own.at[1], pe_in.at[1], es_send.at[1], es_recv.at[1], q, up)
    e_down = copy(pe_own.at[0], pe_in.at[0], es_send.at[0], es_recv.at[0], q, down)

    eye = lax.broadcasted_iota(jnp.int32, (NY, NY), 0) == lax.broadcasted_iota(jnp.int32, (NY, NY), 1)

    row = lax.broadcasted_iota(jnp.int32, (NQ, NY), 0)
    for part, function in ((0, math.cos), (1, math.sin)):
        values = jnp.zeros((NQ, NY), jnp.float32)
        for j in range(NQ):
            values = jnp.where(row == j, RADIUS * function(2.0 * math.pi * (j + 0.5) / NQ), values)
        table[part] = values
    for arrival in arrivals:
        arrival.wait()

    @pl.loop(0, LINES)
    def _(line):
        for part in range(2):
            diagonal = jnp.sum(jnp.where(eye, blocks[part, line], 0.0), axis=0, keepdims=True)
            pack[part, pl.ds(48 + line, 1), :] = diagonal

    for side, line in ((0, 0), (1, LINES - 1)):
        for part in range(2):
            pe_own[side, 8 * part : 8 * part + 8, :] = probes[part, pl.ds(q * OWNED * LINES + line, OWNED, stride=LINES), :]
            pe_own[side, 17 + part : 18 + part, :] = pack[part, 48 + line : 49 + line, :]
        pe_own[side, 16:17, :] = pack[0, 56 + line : 57 + line, :]

    pl.semaphore_wait(barrier, 5 + planes - 1 + 15)

    @pl.when(is_head)
    def _():
        for s in range(2 * len(ORDER)):
            z_head(s).start()

    k_mirror.start()
    p_mirror.start()
    e_up.start()
    e_down.start()

    def prepare(w, probe_re, probe_im, weight, diag_re, diag_im):
        line = d * LINES + zh * (w - FIRST) + (1 - zh) * (SPAN - 1 - FIRST - w)
        inside = jnp.logical_and(line >= 0, line < doms * LINES)
        source_re = weight * probe_re
        source_im = weight * probe_im
        src[w, 0] = source_re
        src[w, 1] = source_im
        denom_re = table[0] * weight - diag_re
        denom_im = table[1] * weight - diag_im
        modulus = denom_re * denom_re + denom_im * denom_im
        inv_re[w] = jnp.where(inside, denom_re / modulus, 0.0)
        inv_im[w] = jnp.where(inside, -denom_im / modulus, 0.0)
        for j in range(NQ):
            g_re = inv_re[w, j : j + 1, :]
            g_im = inv_im[w, j : j + 1, :]
            y1r[w, 8 * j : 8 * j + 8, :] = source_re * g_re - source_im * g_im
            y1i[w, 8 * j : 8 * j + 8, :] = source_re * g_im + source_im * g_re

    def couple(w, ref, line):
        for position in range(6):
            row = zh * position + (1 - zh) * (5 - position)
            for part in range(2):
                cw[w, 6 * part + position : 6 * part + position + 1, :] = ref[part, pl.ds(row * LINES + line, 1), :]

    def prepare_packed(w, line, probe, packed):
        couple(w, packed, line)
        prepare(
            w,
            probe[0, pl.ds(line, OWNED, stride=LINES), :],
            probe[1, pl.ds(line, OWNED, stride=LINES), :],
            packed[0, pl.ds(56 + line, 1), :],
            packed[0, pl.ds(48 + line, 1), :],
            packed[1, pl.ds(48 + line, 1), :],
        )

    def prepare_edge(w, side):
        prepare(w, pe_in[side, 0:8, :], pe_in[side, 8:16, :], pe_in[side, 16:17, :], pe_in[side, 17:18, :], pe_in[side, 18:19, :])

    def own_line(w):
        return zh * (w - FIRST) + (1 - zh) * (SPAN - 1 - FIRST - w)

    def operand(w, block_re, block_im):
        re_high, re_low = split(jnp.where(eye, 0.0, block_re))
        im_high, im_low = split(jnp.where(eye, 0.0, block_im))
        for ref, re, im in ((rhi, re_high, im_high), (rlo, re_low, im_low)):
            ref[w - 3, 0:NY, 0:NY] = re
            ref[w - 3, 0:NY, NY:] = -im
            ref[w - 3, NY:, 0:NY] = im
            ref[w - 3, NY:, NY:] = re

    def image(yr, yi, w, into):
        into[...] = dot3(jnp.concatenate([yr[w], yi[w]], axis=1), rhi[w - 3], rlo[w - 3])

    def finish(yr, yi, w, image_ref, emit, order=range(NQ)):
        c_re = [cw[w, i : i + 1, :] for i in range(6)]
        c_im = [cw[w, 6 + i : 7 + i, :] for i in range(6)]
        source_re = src[w, 0]
        source_im = src[w, 1]
        for j in order:
            part = slice(8 * j, 8 * j + 8)
            a_re = image_ref[part, :NY] + source_re
            a_im = image_ref[part, NY:] + source_im
            for i, offset in enumerate(OFFSETS):
                n_re = yr[w + offset, part, :]
                n_im = yi[w + offset, part, :]
                a_re = a_re + (c_re[i] * n_re - c_im[i] * n_im)
                a_im = a_im + (c_re[i] * n_im + c_im[i] * n_re)
            g_re = inv_re[w, j : j + 1, :]
            g_im = inv_im[w, j : j + 1, :]
            emit(j, g_re * a_re - g_im * a_im, g_re * a_im + g_im * a_re)

    def keep(yr, yi, w):
        def emit(j, re, im):
            yr[w, 8 * j : 8 * j + 8, :] = re
            yi[w, 8 * j : 8 * j + 8, :] = im

        return emit

    def second(w, image_ref):
        finish(y1r, y1i, w, image_ref, keep(y2r, y2i, w))

    def third(w, image_ref):
        finish(y2r, y2i, w, image_ref, keep(y3r, y3i, w))

    def last(w, image_ref):
        line = own_line(w)
        field = {}

        def emit(j, re, im):
            field[j] = (re, im)

        finish(y3r, y3i, w, image_ref, emit, [a + 4 * b for a in range(4) for b in range(4)])
        sum_re = [None] * (2 * MOM)
        sum_im = [None] * (2 * MOM)
        for a in range(4):
            (r0, i0), (r1, i1), (r2, i2), (r3, i3) = (field[a + 4 * b] for b in range(4))
            er, ei, fr, fi = r0 + r2, i0 + i2, r0 - r2, i0 - i2
            gr, gi, hr, hi = r1 + r3, i1 + i3, r1 - r3, i1 - i3
            groups = ((er + gr, ei + gi), (fr - hi, fi + hr), (er - gr, ei - gi), (fr + hi, fi - hr))
            for k in range(2 * MOM):
                x_re, x_im = groups[(k + 1) % 4]
                w_re, w_im = WEIGHTS[k][a]
                t_re = w_re * x_re - w_im * x_im
                t_im = w_re * x_im + w_im * x_re
                sum_re[k] = t_re if a == 0 else sum_re[k] + t_re
                sum_im[k] = t_im if a == 0 else sum_im[k] + t_im
        for k in range(MOM):
            mom_ref[pl.ds(k * 16 + line, OWNED, stride=64), :] = sum_re[k]
            mom_ref[pl.ds(k * 16 + 8 + line, OWNED, stride=64), :] = sum_im[k]
        m_high, m_low = split(jnp.concatenate(sum_re + sum_im, axis=0))
        probe_lines = jnp.concatenate([probes[part, pl.ds(line, 64, stride=LINES), :] for part in range(2)], axis=0)
        gram[...] += dot3(probe_lines, m_high, m_low)

    def pairs(yr, yi, step, first, count):
        image(yr, yi, first, ima)

        @pl.loop(0, count // 2)
        def _(i):
            w = first + 2 * i
            image(yr, yi, w + 1, imb)
            step(w, ima)
            image(yr, yi, jnp.minimum(w + 2, first + count - 1), ima)
            step(w + 1, imb)

        if count % 2:
            step(first + count - 1, ima)

    def relay(s):
        for piece in (2 * s, 2 * s + 1):
            z_copy(piece).wait_recv()
            pl.when(head == 0)(z_copy(piece).start)

        if ORDER[s] >= 2:
            y_copy(LINES - 1 - ORDER[s]).start()

        if ORDER[s] < RIM:
            sz_copy(ORDER[s], c).start()

    def pass_small():
        k_mirror.wait_recv()
        y_pack().start()
        sz_pack(c).start()
        p_mirror.wait_recv()
        p_next.start()

    def prepare_z():
        sz_pack(o).wait_recv()
        e_down.wait_recv()
        e_up.wait_recv()

        @pl.loop(0, LINES)
        def _(t):
            prepare_packed(FIRST - 1 - t, (1 - zh) * t + zh * (LINES - 1 - t), pz, zk)

        prepare_edge(0, zh)

    def share_y():
        y_pack().wait_recv()
        sy_pack(c).start()

    def prepare_y():
        p_next.wait_recv()
        sy_pack(o).wait_recv()

        @pl.loop(0, LINES)
        def _(u):
            prepare_packed(FIRST + LINES + u, (1 - zh) * (LINES - 1 - u) + zh * u, py, yk)

        prepare_edge(SPAN - 1, 1 - zh)

    gram[...] = jnp.zeros_like(gram)

    @pl.loop(FIRST, FIRST + LINES)
    def _(w):
        line = own_line(w)
        couple(w, pack, line)
        prepare(
            w,
            probes[0, pl.ds(q * OWNED * LINES + line, OWNED, stride=LINES), :],
            probes[1, pl.ds(q * OWNED * LINES + line, OWNED, stride=LINES), :],
            pack[0, pl.ds(56 + line, 1), :],
            pack[0, pl.ds(48 + line, 1), :],
            pack[1, pl.ds(48 + line, 1), :],
        )
        operand(w, blocks[0, line], blocks[1, line])

    def z_pair(t):
        w = FIRST - 1 - t
        sz_copy(t, o).wait_recv()
        operand(w, zb[0, t], zb[1, t])
        image(y1r, y1i, w, ima)
        sz_copy(t + 1, o).wait_recv()
        operand(w - 1, zb[0, t + 1], zb[1, t + 1])
        image(y1r, y1i, w - 1, imb)
        second(w, ima)
        second(w - 1, imb)

    def share(u):
        y_copy(u).wait_recv()
        sy_copy(u, c).start()

    def y_line(u):
        sy_copy(u, o).wait_recv()
        w = FIRST + LINES + u
        image(y2r, y2i, w - 3, imb)
        operand(w, yb[0, u], yb[1, u])
        image(y1r, y1i, w, ima)
        second(w, ima)
        third(w - 3, imb)

    own = functools.partial(pairs, y1r, y1i, second)

    @pl.when(jnp.logical_not(far))
    def _():
        for s in range(4):
            relay(s)
        pass_small()
        relay(4)
        prepare_z()
        relay(5)
        own(FIRST, 2)
        relay(6)
        own(FIRST + 2, 2)
        relay(7)
        share_y()
        prepare_y()
        own(FIRST + 4, 4)
        for u in range(3):
            share(u)
        z_pair(0)
        pairs(y2r, y2i, third, FIRST + 1, 4)
        pl.loop(0, 2)(y_line)
        z_pair(4)
        y_line(2)

    @pl.when(jnp.logical_and(far, head == 0))
    def _():
        pass_small()
        for s in range(3):
            relay(s)
        prepare_z()
        relay(3)
        own(FIRST, 2)
        relay(4)
        own(FIRST + 2, 2)
        relay(5)
        share_y()
        relay(6)
        relay(7)
        prepare_y()
        share(0)
        share(1)
        own(FIRST + 4, 4)
        z_pair(0)
        share(2)
        pairs(y2r, y2i, third, FIRST + 1, 4)
        z_pair(4)
        pl.loop(0, 3)(y_line)

    @pl.when(is_head)
    def _():
        pass_small()
        prepare_z()
        own(FIRST, 4)
        relay(0)
        relay(1)
        share_y()
        relay(2)
        prepare_y()
        relay(3)
        own(FIRST + 4, 4)
        relay(4)
        share(0)
        z_pair(0)
        relay(5)
        pairs(y2r, y2i, third, FIRST + 1, 4)
        relay(6)
        share(1)
        z_pair(4)
        y_line(0)
        relay(7)
        share(2)
        pl.loop(1, 3)(y_line)

    share(3)
    z_pair(2)
    pairs(y2r, y2i, third, FIRST - 3, 4)
    pairs(y3r, y3i, last, FIRST, 5)

    @pl.loop(3, RIM)
    def _(u):
        @pl.when(u < RIM - 1)
        def _():
            y_copy(u + 1).wait_recv()
            sy_copy(u + 1, c).start()

        sy_copy(u, o).wait_recv()
        w = FIRST + LINES + u
        image(y3r, y3i, w - 6, imc)
        image(y2r, y2i, w - 3, imb)
        operand(w, yb[0, u], yb[1, u])
        image(y1r, y1i, w, ima)
        second(w, ima)
        third(w - 3, imb)
        last(w - 6, imc)

    lane = lax.broadcasted_iota(jnp.int32, (64, 128), 1)
    other = pltpu.roll(gram[64:, :], 64, 1)
    scale = 1.0 / float(doms * LINES * NY)
    partial = scale * (gram[:64, :] + jnp.where(lane < 64, other, -other))
    for i in range(planes):
        mine[i] = partial[i * rows : (i + 1) * rows, :]

    def dev(quad, dom):
        return {"quad": quad, "dom": dom}

    def plane_copy(i):
        to = lax.rem(m + i, planes)
        return pltpu.make_async_remote_copy(
            src_ref=mine.at[to], dst_ref=gathered.at[i], send_sem=s1.at[i], recv_sem=r1.at[i],
            device_id=dev(q, to * 2 + zh), device_id_type=pl.DeviceIdType.MESH,
        )

    def column_copy(i):
        to = lax.rem(slot + i, 16)
        return pltpu.make_async_remote_copy(
            src_ref=column.at[slot], dst_ref=column.at[slot], send_sem=s2.at[i], recv_sem=r2.at[i],
            device_id=dev(lax.rem(to, 8), 2 * m + lax.div(to, 8)), device_id_type=pl.DeviceIdType.MESH,
        )

    def column_arrived(i):
        come = lax.rem(slot + 16 - i, 16)
        return pltpu.make_async_remote_copy(
            src_ref=column.at[come], dst_ref=column.at[come], send_sem=s2.at[i], recv_sem=r2.at[i],
            device_id=dev(lax.rem(come, 8), 2 * m + lax.div(come, 8)), device_id_type=pl.DeviceIdType.MESH,
        )

    def full_copy(i):
        to = lax.rem(m + i, planes)
        return pltpu.make_async_remote_copy(
            src_ref=total, dst_ref=full.at[m], send_sem=s3.at[i], recv_sem=r3.at[i],
            device_id=dev(q, to * 2 + zh), device_id_type=pl.DeviceIdType.MESH,
        )

    def full_arrived(i):
        come = lax.rem(m + planes - i, planes)
        return pltpu.make_async_remote_copy(
            src_ref=total, dst_ref=full.at[come], send_sem=s3.at[i], recv_sem=r3.at[i],
            device_id=dev(q, come * 2 + zh), device_id_type=pl.DeviceIdType.MESH,
        )

    for i in PLANE_ORDER:
        plane_copy(i).start()

    gathered[0] = mine[m]

    for i in range(1, planes):
        plane_copy(i).wait_recv()

    column[slot] = functools.reduce(lambda a, b: a + b, [gathered[i] for i in range(planes)])

    for i in COLUMN_ORDER:
        column_copy(i).start()

    for i in range(1, 16):
        column_arrived(i).wait_recv()

    group = lax.div(lax.broadcasted_iota(jnp.int32, (rows, NY), 1), 8)
    sums = [column[i] + column[8 + i] for i in range(8)]
    for pair in range(8):
        value = jnp.zeros((rows, NY), jnp.float32)
        for half in range(2):
            for i in range(8):
                to = 8 * half + i
                shift = (to - 2 * pair - half) % 16 * 8
                moved = pltpu.roll(sums[i], shift, 1) if shift else sums[i]
                value = jnp.where(group == to, moved, value)
        total[pair] = value

    for i in PLANE_ORDER:
        full_copy(i).start()

    full[m] = total[...]

    for i in range(1, planes):
        full_arrived(i).wait_recv()

    for i in range(planes):
        for pair in range(8):
            value = full[i, pair]
            out_ref[2 * pair, rows * i : rows * (i + 1), :] = value[:, :64]
            out_ref[2 * pair + 1, rows * i : rows * (i + 1), :] = value[:, 64:]

    @pl.loop(1, planes)
    def _(i):
        plane_copy(i).wait_send()
        full_copy(i).wait_send()

    @pl.loop(1, 16)
    def _(i):
        column_copy(i).wait_send()

    k_mirror.wait_send()
    p_mirror.wait_send()
    p_next.wait_send()
    e_up.wait_send()
    e_down.wait_send()
    for s in range(2 * len(ORDER)):
        z_copy(s).wait_send()
    y_pack().wait_send()
    sz_pack(c).wait_send()
    sy_pack(c).wait_send()
    for i in range(RIM):
        y_copy(i).wait_send()
        sz_copy(i, c).wait_send()
        sy_copy(i, c).wait_send()


def on_device(doms, probes, mass_weights, blocks, couplings):
    f32 = jnp.float32
    planes = doms // 2
    rows = 64 // planes
    vmem = pl.BlockSpec(memory_space=pltpu.VMEM)
    dma = pltpu.SemaphoreType.DMA
    moments, projected = pl.pallas_call(
        functools.partial(sweep_kernel, doms),
        out_shape=(jax.ShapeDtypeStruct((512, NY), f32), jax.ShapeDtypeStruct((16, 64, 64), f32)),
        in_specs=[pl.BlockSpec(memory_space=pl.ANY)] * 4,
        out_specs=(vmem, vmem),
        scratch_shapes=[
            pltpu.VMEM((2, 512, NY), f32),
            pltpu.VMEM((2, LINES, NY, NY), f32),
            pltpu.VMEM((2, NQ, NY), f32),
            pltpu.VMEM((2, LINES, NY, NY), f32),
            pltpu.VMEM((2, RIM, NY, NY), f32),
            pltpu.VMEM((2, 64, NY), f32),
            pltpu.VMEM((2, 64, NY), f32),
            pltpu.VMEM((2, 64, NY), f32),
            pltpu.VMEM((2, 64, NY), f32),
            pltpu.VMEM((2, 24, NY), f32),
            pltpu.VMEM((2, 24, NY), f32),
            pltpu.VMEM((2, 64, NY), f32),
            pltpu.VMEM((SPAN, NQ, NY), f32),
            pltpu.VMEM((SPAN, NQ, NY), f32),
            pltpu.VMEM((SPAN, 2, OWNED, NY), f32),
            pltpu.VMEM((SPAN, 16, NY), f32),
            pltpu.VMEM((20, 2 * NY, 2 * NY), jnp.bfloat16),
            pltpu.VMEM((20, 2 * NY, 2 * NY), jnp.bfloat16),
        ]
        + [pltpu.VMEM((SPAN, NQ * OWNED, NY), f32)] * 6
        + [pltpu.VMEM((NY, 2 * NY), f32)] * 3
        + [
            pltpu.VMEM((NY, NY), f32),
            pltpu.VMEM((planes, rows, NY), f32),
            pltpu.VMEM((planes, rows, NY), f32),
            pltpu.VMEM((16, rows, NY), f32),
            pltpu.VMEM((8, rows, NY), f32),
            pltpu.VMEM((planes, 8, rows, NY), f32),
        ]
        + [dma((5,))]
        + [dma((16,))] * 2
        + [dma((7,))] * 6
        + [dma((3,))] * 2
        + [dma((2,))] * 2
        + [dma((16,))] * 6,
        compiler_params=pltpu.CompilerParams(collective_id=0, has_side_effects=True, vmem_limit_bytes=60 * 1024 * 1024),
    )(probes.reshape(2, 512, NY), mass_weights, blocks, couplings.reshape(2, 48, NY))
    return moments.reshape(OWNED, MOM, 2, LINES, NY), projected.reshape(2, 8, 64, 64)


def solution(mesh):
    return jax.shard_map(
        functools.partial(on_device, mesh.shape["dom"]),
        mesh=mesh,
        in_specs=(P(None, None, "dom", None), P("dom", None), P(None, "dom", None, None), P(None, None, "dom", None)),
        out_specs=(P("quad", None, None, "dom", None), P()),
        check_vma=False,
    )
```

```python
import functools
import math

import jax
import jax.numpy as jnp
import numpy as np
from jax import lax
from jax.experimental import pallas as pl
from jax.experimental.pallas import tpu as pltpu
from jax.sharding import PartitionSpec as P

NQ = 16
MOM = 4
RADIUS = 2.0
OFFSETS = (-3, -2, -1, 1, 2, 3)
LINES = 8
OWNED = 8
NY = 128
FIRST = 9
SPAN = 26
ORDER = (7, 0, 6, 1, 5, 4, 3, 2)
RIM = 6
PLANE_ORDER = (10, 6, 9, 11, 14, 2, 8, 5, 7, 13, 3, 15, 1, 12, 4)
COLUMN_ORDER = (8, 7, 9, 6, 10, 5, 11, 4, 12, 3, 13, 2, 14, 15, 1)
NT = (((1,), (1,)), ((), ()))


def weights():
    theta = 2.0 * math.pi * (np.arange(NQ) + 0.5) / NQ
    return [[(RADIUS / NQ * math.cos(k * theta[a]), RADIUS / NQ * math.sin(k * theta[a])) for a in range(4)] for k in range(1, 2 * MOM + 1)]


WEIGHTS = weights()


def split(value):
    high = value.astype(jnp.bfloat16)
    low = (value - high.astype(jnp.float32)).astype(jnp.bfloat16)
    return high, low


def dot3(lhs, rhs_high, rhs_low):
    dot = functools.partial(lax.dot_general, dimension_numbers=NT, preferred_element_type=jnp.float32)
    high, low = split(lhs)
    count = lhs.shape[0]
    both = dot(jnp.concatenate([high, low], axis=0), rhs_high)
    return both[:count] + both[count:] + dot(high, rhs_low)


def sweep_kernel(
    doms, probes_hbm, mass_hbm, blocks_hbm, coup_hbm, mom_ref, out_ref,
    probes, blocks, table, zb, yb, zk, yk, pz, py, pe_own, pe_in, pack, inv_re, inv_im, src, cw, rhi, rlo,
    y1r, y1i, y2r, y2i, y3r, y3i, ima, imb, imc, gram, mine, gathered, column, total, full,
    in_sem, zs_send, zs_recv, zk_send, ys_send, ys_recv, sz_send, sz_recv, sy_send, sy_recv, ps_send, ps_recv, es_send, es_recv,
    s1, r1, s2, r2, s3, r3,
):
    q = lax.axis_index("quad")
    d = lax.axis_index("dom")
    c = lax.rem(q, 2)
    o = 1 - c
    zl = lax.div(q, 2)
    zh = lax.rem(d, 2)
    flip = d + 1 - 2 * zh
    up = lax.rem(d + 2, doms)
    down = lax.rem(d + doms - 2, doms)
    y_to = lax.rem(d + 2 - 4 * zh + doms, doms)
    at_top = lax.div(q + 2, 8)
    at_bottom = 1 - lax.div(q + 6, 8)
    head = (1 - c) * at_top + c * at_bottom
    q_to = lax.rem(q + 8 + 2 - 4 * c, 8)
    d_to = d + head * (1 - 2 * zh)
    sib = q + 1 - 2 * c
    mirror = 2 * (3 - zl) + c
    is_head = head == 1
    depth = c * (3 - zl) + (1 - c) * zl
    far = lax.div(depth, 2) == 1
    q_skip = lax.rem(q + 8 + 4 - 8 * c, 8)
    planes = doms // 2
    rows = 64 // planes
    m = lax.div(d, 2)
    slot = zh * 8 + q

    arrivals = [
        pltpu.make_async_copy(coup_hbm, pack.at[:, pl.ds(0, 48), :], in_sem.at[0]),
        pltpu.make_async_copy(mass_hbm, pack.at[0, pl.ds(56, 8), :], in_sem.at[1]),
        pltpu.make_async_copy(mass_hbm, pack.at[1, pl.ds(56, 8), :], in_sem.at[2]),
        pltpu.make_async_copy(probes_hbm, probes, in_sem.at[3]),
        pltpu.make_async_copy(blocks_hbm, blocks, in_sem.at[4]),
    ]
    for arrival in arrivals:
        arrival.start()

    barrier = pltpu.get_barrier_semaphore()

    def greet(quad, dom):
        pl.semaphore_signal(barrier, inc=1, device_id={"quad": quad, "dom": dom}, device_id_type=pl.DeviceIdType.MESH)

    @pl.loop(1, planes)
    def _(i):
        greet(q, lax.rem(m + i, planes) * 2 + zh)

    @pl.loop(1, 16)
    def _(i):
        to = lax.rem(slot + i, 16)
        greet(lax.rem(to, 8), 2 * m + lax.div(to, 8))

    def copy(source, target, send, recv, quad, dom):
        return pltpu.make_async_remote_copy(
            src_ref=source, dst_ref=target, send_sem=send, recv_sem=recv,
            device_id={"quad": quad, "dom": dom}, device_id_type=pl.DeviceIdType.MESH,
        )

    def z_copy(s):
        t = ORDER[s // 2]
        piece = zb.at[c, t, pl.ds(s % 2 * 64, 64), :]
        return copy(piece, piece, zs_send.at[s], zs_recv.at[s], q_to, d_to)

    def z_skip(s):
        t = ORDER[s // 2]
        piece = zb.at[c, t, pl.ds(s % 2 * 64, 64), :]
        return copy(piece, piece, zk_send.at[s], zs_recv.at[s], q_skip, d)

    def z_head(s):
        t = ORDER[s // 2]
        half = pl.ds(s % 2 * 64, 64)
        line = zh * t + (1 - zh) * (LINES - 1 - t)
        return copy(blocks_hbm.at[c, line, half, :], zb.at[c, t, half, :], zs_send.at[s], zs_recv.at[s], q_to, d_to)

    def y_pack():
        return copy(zk.at[c], yk.at[c], ys_send.at[RIM], ys_recv.at[RIM], q, y_to)

    def y_copy(u):
        return copy(zb.at[c, LINES - 1 - u], yb.at[c, u], ys_send.at[u], ys_recv.at[u], q, y_to)

    def sz_pack(part):
        return copy(zk.at[part], zk.at[part], sz_send.at[RIM], sz_recv.at[RIM], sib, d)

    def sz_copy(t, part):
        return copy(zb.at[part, t], zb.at[part, t], sz_send.at[t], sz_recv.at[t], sib, d)

    def sy_pack(part):
        return copy(yk.at[part], yk.at[part], sy_send.at[RIM], sy_recv.at[RIM], sib, d)

    def sy_copy(u, part):
        return copy(yb.at[part, u], yb.at[part, u], sy_send.at[u], sy_recv.at[u], sib, d)

    k_mirror = copy(pack.at[c], zk.at[c], ps_send.at[2], ps_recv.at[2], mirror, flip)
    p_mirror = copy(probes_hbm.at[:, pl.ds(mirror * OWNED * LINES, OWNED * LINES), :], pz, ps_send.at[0], ps_recv.at[0], mirror, flip)
    p_next = copy(pz, py, ps_send.at[1], ps_recv.at[1], q, y_to)
    e_up = copy(pe_own.at[1], pe_in.at[1], es_send.at[1], es_recv.at[1], q, up)
    e_down = copy(pe_own.at[0], pe_in.at[0], es_send.at[0], es_recv.at[0], q, down)

    eye = lax.broadcasted_iota(jnp.int32, (NY, NY), 0) == lax.broadcasted_iota(jnp.int32, (NY, NY), 1)

    row = lax.broadcasted_iota(jnp.int32, (NQ, NY), 0)
    for part, function in ((0, math.cos), (1, math.sin)):
        values = jnp.zeros((NQ, NY), jnp.float32)
        for j in range(NQ):
            values = jnp.where(row == j, RADIUS * function(2.0 * math.pi * (j + 0.5) / NQ), values)
        table[part] = values
    for arrival in arrivals:
        arrival.wait()

    @pl.loop(0, LINES)
    def _(line):
        for part in range(2):
            diagonal = jnp.sum(jnp.where(eye, blocks[part, line], 0.0), axis=0, keepdims=True)
            pack[part, pl.ds(48 + line, 1), :] = diagonal

    for side, line in ((0, 0), (1, LINES - 1)):
        for part in range(2):
            pe_own[side, 8 * part : 8 * part + 8, :] = probes[part, pl.ds(q * OWNED * LINES + line, OWNED, stride=LINES), :]
            pe_own[side, 17 + part : 18 + part, :] = pack[part, 48 + line : 49 + line, :]
        pe_own[side, 16:17, :] = pack[0, 56 + line : 57 + line, :]

    pl.semaphore_wait(barrier, planes - 1 + 15)

    @pl.when(is_head)
    def _():
        for s in range(2 * len(ORDER)):
            z_head(s).start()

    k_mirror.start()
    p_mirror.start()
    e_up.start()
    e_down.start()

    def prepare(w, probe_re, probe_im, weight, diag_re, diag_im):
        line = d * LINES + zh * (w - FIRST) + (1 - zh) * (SPAN - 1 - FIRST - w)
        inside = jnp.logical_and(line >= 0, line < doms * LINES)
        source_re = weight * probe_re
        source_im = weight * probe_im
        src[w, 0] = source_re
        src[w, 1] = source_im
        denom_re = table[0] * weight - diag_re
        denom_im = table[1] * weight - diag_im
        modulus = denom_re * denom_re + denom_im * denom_im
        inv_re[w] = jnp.where(inside, denom_re / modulus, 0.0)
        inv_im[w] = jnp.where(inside, -denom_im / modulus, 0.0)
        for j in range(NQ):
            g_re = inv_re[w, j : j + 1, :]
            g_im = inv_im[w, j : j + 1, :]
            y1r[w, 8 * j : 8 * j + 8, :] = source_re * g_re - source_im * g_im
            y1i[w, 8 * j : 8 * j + 8, :] = source_re * g_im + source_im * g_re

    def couple(w, ref, line):
        for position in range(6):
            row = zh * position + (1 - zh) * (5 - position)
            for part in range(2):
                cw[w, 6 * part + position : 6 * part + position + 1, :] = ref[part, pl.ds(row * LINES + line, 1), :]

    def prepare_packed(w, line, probe, packed):
        couple(w, packed, line)
        prepare(
            w,
            probe[0, pl.ds(line, OWNED, stride=LINES), :],
            probe[1, pl.ds(line, OWNED, stride=LINES), :],
            packed[0, pl.ds(56 + line, 1), :],
            packed[0, pl.ds(48 + line, 1), :],
            packed[1, pl.ds(48 + line, 1), :],
        )

    def prepare_edge(w, side):
        prepare(w, pe_in[side, 0:8, :], pe_in[side, 8:16, :], pe_in[side, 16:17, :], pe_in[side, 17:18, :], pe_in[side, 18:19, :])

    def own_line(w):
        return zh * (w - FIRST) + (1 - zh) * (SPAN - 1 - FIRST - w)

    def operand(w, block_re, block_im):
        re_high, re_low = split(jnp.where(eye, 0.0, block_re))
        im_high, im_low = split(jnp.where(eye, 0.0, block_im))
        for ref, re, im in ((rhi, re_high, im_high), (rlo, re_low, im_low)):
            ref[w - 3, 0:NY, 0:NY] = re
            ref[w - 3, 0:NY, NY:] = -im
            ref[w - 3, NY:, 0:NY] = im
            ref[w - 3, NY:, NY:] = re

    def image(yr, yi, w, into):
        into[...] = dot3(jnp.concatenate([yr[w], yi[w]], axis=1), rhi[w - 3], rlo[w - 3])

    def finish(yr, yi, w, image_ref, emit, order=range(NQ)):
        c_re = [cw[w, i : i + 1, :] for i in range(6)]
        c_im = [cw[w, 6 + i : 7 + i, :] for i in range(6)]
        source_re = src[w, 0]
        source_im = src[w, 1]
        for j in order:
            part = slice(8 * j, 8 * j + 8)
            a_re = image_ref[part, :NY] + source_re
            a_im = image_ref[part, NY:] + source_im
            for i, offset in enumerate(OFFSETS):
                n_re = yr[w + offset, part, :]
                n_im = yi[w + offset, part, :]
                a_re = a_re + (c_re[i] * n_re - c_im[i] * n_im)
                a_im = a_im + (c_re[i] * n_im + c_im[i] * n_re)
            g_re = inv_re[w, j : j + 1, :]
            g_im = inv_im[w, j : j + 1, :]
            emit(j, g_re * a_re - g_im * a_im, g_re * a_im + g_im * a_re)

    def keep(yr, yi, w):
        def emit(j, re, im):
            yr[w, 8 * j : 8 * j + 8, :] = re
            yi[w, 8 * j : 8 * j + 8, :] = im

        return emit

    def second(w, image_ref):
        finish(y1r, y1i, w, image_ref, keep(y2r, y2i, w))

    def third(w, image_ref):
        finish(y2r, y2i, w, image_ref, keep(y3r, y3i, w))

    def last(w, image_ref):
        line = own_line(w)
        field = {}

        def emit(j, re, im):
            field[j] = (re, im)

        finish(y3r, y3i, w, image_ref, emit, [a + 4 * b for a in range(4) for b in range(4)])
        sum_re = [None] * (2 * MOM)
        sum_im = [None] * (2 * MOM)
        for a in range(4):
            (r0, i0), (r1, i1), (r2, i2), (r3, i3) = (field[a + 4 * b] for b in range(4))
            er, ei, fr, fi = r0 + r2, i0 + i2, r0 - r2, i0 - i2
            gr, gi, hr, hi = r1 + r3, i1 + i3, r1 - r3, i1 - i3
            groups = ((er + gr, ei + gi), (fr - hi, fi + hr), (er - gr, ei - gi), (fr + hi, fi - hr))
            for k in range(2 * MOM):
                x_re, x_im = groups[(k + 1) % 4]
                w_re, w_im = WEIGHTS[k][a]
                t_re = w_re * x_re - w_im * x_im
                t_im = w_re * x_im + w_im * x_re
                sum_re[k] = t_re if a == 0 else sum_re[k] + t_re
                sum_im[k] = t_im if a == 0 else sum_im[k] + t_im
        for k in range(MOM):
            mom_ref[pl.ds(k * 16 + line, OWNED, stride=64), :] = sum_re[k]
            mom_ref[pl.ds(k * 16 + 8 + line, OWNED, stride=64), :] = sum_im[k]
        m_high, m_low = split(jnp.concatenate(sum_re + sum_im, axis=0))
        probe_lines = jnp.concatenate([probes[part, pl.ds(line, 64, stride=LINES), :] for part in range(2)], axis=0)
        gram[...] += dot3(probe_lines, m_high, m_low)

    def pairs(yr, yi, step, first, count):
        image(yr, yi, first, ima)

        @pl.loop(0, count // 2)
        def _(i):
            w = first + 2 * i
            image(yr, yi, w + 1, imb)
            step(w, ima)
            image(yr, yi, jnp.minimum(w + 2, first + count - 1), ima)
            step(w + 1, imb)

        if count % 2:
            step(first + count - 1, ima)

    def relay(s):
        for piece in (2 * s, 2 * s + 1):
            z_copy(piece).wait_recv()
            first = z_skip(piece), z_copy(piece)

            @pl.when(depth == 0)
            def _():
                first[0].start()
                first[1].start()

            pl.when(depth == 2)(first[1].start)

        if ORDER[s] >= 2:
            y_copy(LINES - 1 - ORDER[s]).start()

        if ORDER[s] < RIM:
            sz_copy(ORDER[s], c).start()

    def pass_small():
        k_mirror.wait_recv()
        y_pack().start()
        sz_pack(c).start()
        p_mirror.wait_recv()
        p_next.start()

    def prepare_z():
        sz_pack(o).wait_recv()
        e_down.wait_recv()
        e_up.wait_recv()

        @pl.loop(0, LINES)
        def _(t):
            prepare_packed(FIRST - 1 - t, (1 - zh) * t + zh * (LINES - 1 - t), pz, zk)

        prepare_edge(0, zh)

    def share_y():
        y_pack().wait_recv()
        sy_pack(c).start()

    def prepare_y():
        p_next.wait_recv()
        sy_pack(o).wait_recv()

        @pl.loop(0, LINES)
        def _(u):
            prepare_packed(FIRST + LINES + u, (1 - zh) * (LINES - 1 - u) + zh * u, py, yk)

        prepare_edge(SPAN - 1, 1 - zh)

    gram[...] = jnp.zeros_like(gram)

    @pl.loop(FIRST, FIRST + LINES)
    def _(w):
        line = own_line(w)
        couple(w, pack, line)
        prepare(
            w,
            probes[0, pl.ds(q * OWNED * LINES + line, OWNED, stride=LINES), :],
            probes[1, pl.ds(q * OWNED * LINES + line, OWNED, stride=LINES), :],
            pack[0, pl.ds(56 + line, 1), :],
            pack[0, pl.ds(48 + line, 1), :],
            pack[1, pl.ds(48 + line, 1), :],
        )
        operand(w, blocks[0, line], blocks[1, line])

    def z_pair(t):
        w = FIRST - 1 - t
        sz_copy(t, o).wait_recv()
        operand(w, zb[0, t], zb[1, t])
        image(y1r, y1i, w, ima)
        sz_copy(t + 1, o).wait_recv()
        operand(w - 1, zb[0, t + 1], zb[1, t + 1])
        image(y1r, y1i, w - 1, imb)
        second(w, ima)
        second(w - 1, imb)

    def share(u):
        y_copy(u).wait_recv()
        sy_copy(u, c).start()

    def y_line(u):
        sy_copy(u, o).wait_recv()
        w = FIRST + LINES + u
        image(y2r, y2i, w - 3, imb)
        operand(w, yb[0, u], yb[1, u])
        image(y1r, y1i, w, ima)
        second(w, ima)
        third(w - 3, imb)

    own = functools.partial(pairs, y1r, y1i, second)

    @pl.when(jnp.logical_not(far))
    def _():
        for s in range(4):
            relay(s)
        pass_small()
        relay(4)
        prepare_z()
        relay(5)
        own(FIRST, 2)
        relay(6)
        own(FIRST + 2, 2)
        relay(7)
        share_y()
        prepare_y()
        own(FIRST + 4, 4)
        for u in range(3):
            share(u)
        z_pair(0)
        pairs(y2r, y2i, third, FIRST + 1, 4)
        pl.loop(0, 2)(y_line)
        z_pair(4)
        y_line(2)

    @pl.when(jnp.logical_and(far, head == 0))
    def _():
        pass_small()
        for s in range(3):
            relay(s)
        prepare_z()
        relay(3)
        own(FIRST, 2)
        relay(4)
        own(FIRST + 2, 2)
        relay(5)
        share_y()
        relay(6)
        relay(7)
        prepare_y()
        share(0)
        share(1)
        own(FIRST + 4, 4)
        z_pair(0)
        share(2)
        pairs(y2r, y2i, third, FIRST + 1, 4)
        z_pair(4)
        pl.loop(0, 3)(y_line)

    @pl.when(is_head)
    def _():
        pass_small()
        prepare_z()
        own(FIRST, 4)
        relay(0)
        relay(1)
        share_y()
        relay(2)
        prepare_y()
        relay(3)
        own(FIRST + 4, 4)
        relay(4)
        share(0)
        z_pair(0)
        relay(5)
        pairs(y2r, y2i, third, FIRST + 1, 4)
        relay(6)
        share(1)
        z_pair(4)
        y_line(0)
        relay(7)
        share(2)
        pl.loop(1, 3)(y_line)

    share(3)
    z_pair(2)
    pairs(y2r, y2i, third, FIRST - 3, 4)
    pairs(y3r, y3i, last, FIRST, 5)

    @pl.loop(3, RIM)
    def _(u):
        @pl.when(u < RIM - 1)
        def _():
            y_copy(u + 1).wait_recv()
            sy_copy(u + 1, c).start()

        sy_copy(u, o).wait_recv()
        w = FIRST + LINES + u
        image(y3r, y3i, w - 6, imc)
        image(y2r, y2i, w - 3, imb)
        operand(w, yb[0, u], yb[1, u])
        image(y1r, y1i, w, ima)
        second(w, ima)
        third(w - 3, imb)
        last(w - 6, imc)

    lane = lax.broadcasted_iota(jnp.int32, (64, 128), 1)
    other = pltpu.roll(gram[64:, :], 64, 1)
    scale = 1.0 / float(doms * LINES * NY)
    partial = scale * (gram[:64, :] + jnp.where(lane < 64, other, -other))
    for i in range(planes):
        mine[i] = partial[i * rows : (i + 1) * rows, :]

    def dev(quad, dom):
        return {"quad": quad, "dom": dom}

    def plane_copy(i):
        to = lax.rem(m + i, planes)
        return pltpu.make_async_remote_copy(
            src_ref=mine.at[to], dst_ref=gathered.at[i], send_sem=s1.at[i], recv_sem=r1.at[i],
            device_id=dev(q, to * 2 + zh), device_id_type=pl.DeviceIdType.MESH,
        )

    def column_copy(i):
        to = lax.rem(slot + i, 16)
        return pltpu.make_async_remote_copy(
            src_ref=column.at[slot], dst_ref=column.at[slot], send_sem=s2.at[i], recv_sem=r2.at[i],
            device_id=dev(lax.rem(to, 8), 2 * m + lax.div(to, 8)), device_id_type=pl.DeviceIdType.MESH,
        )

    def column_arrived(i):
        come = lax.rem(slot + 16 - i, 16)
        return pltpu.make_async_remote_copy(
            src_ref=column.at[come], dst_ref=column.at[come], send_sem=s2.at[i], recv_sem=r2.at[i],
            device_id=dev(lax.rem(come, 8), 2 * m + lax.div(come, 8)), device_id_type=pl.DeviceIdType.MESH,
        )

    def full_copy(i):
        to = lax.rem(m + i, planes)
        return pltpu.make_async_remote_copy(
            src_ref=total, dst_ref=full.at[m], send_sem=s3.at[i], recv_sem=r3.at[i],
            device_id=dev(q, to * 2 + zh), device_id_type=pl.DeviceIdType.MESH,
        )

    def full_arrived(i):
        come = lax.rem(m + planes - i, planes)
        return pltpu.make_async_remote_copy(
            src_ref=total, dst_ref=full.at[come], send_sem=s3.at[i], recv_sem=r3.at[i],
            device_id=dev(q, come * 2 + zh), device_id_type=pl.DeviceIdType.MESH,
        )

    for i in PLANE_ORDER:
        plane_copy(i).start()

    gathered[0] = mine[m]

    for i in range(1, planes):
        plane_copy(i).wait_recv()

    column[slot] = functools.reduce(lambda a, b: a + b, [gathered[i] for i in range(planes)])

    for i in COLUMN_ORDER:
        column_copy(i).start()

    for i in range(1, 16):
        column_arrived(i).wait_recv()

    group = lax.div(lax.broadcasted_iota(jnp.int32, (rows, NY), 1), 8)
    sums = [column[i] + column[8 + i] for i in range(8)]
    for pair in range(8):
        value = jnp.zeros((rows, NY), jnp.float32)
        for half in range(2):
            for i in range(8):
                to = 8 * half + i
                shift = (to - 2 * pair - half) % 16 * 8
                moved = pltpu.roll(sums[i], shift, 1) if shift else sums[i]
                value = jnp.where(group == to, moved, value)
        total[pair] = value

    for i in PLANE_ORDER:
        full_copy(i).start()

    full[m] = total[...]

    for i in range(1, planes):
        full_arrived(i).wait_recv()

    for i in range(planes):
        for pair in range(8):
            value = full[i, pair]
            out_ref[2 * pair, rows * i : rows * (i + 1), :] = value[:, :64]
            out_ref[2 * pair + 1, rows * i : rows * (i + 1), :] = value[:, 64:]

    @pl.loop(1, planes)
    def _(i):
        plane_copy(i).wait_send()
        full_copy(i).wait_send()

    @pl.loop(1, 16)
    def _(i):
        column_copy(i).wait_send()

    k_mirror.wait_send()
    p_mirror.wait_send()
    p_next.wait_send()
    e_up.wait_send()
    e_down.wait_send()

    @pl.when(depth != 1)
    def _():
        for s in range(2 * len(ORDER)):
            z_copy(s).wait_send()

    @pl.when(depth == 0)
    def _():
        for s in range(2 * len(ORDER)):
            z_skip(s).wait_send()

    y_pack().wait_send()
    sz_pack(c).wait_send()
    sy_pack(c).wait_send()
    for i in range(RIM):
        y_copy(i).wait_send()
        sz_copy(i, c).wait_send()
        sy_copy(i, c).wait_send()


def on_device(doms, probes, mass_weights, blocks, couplings):
    f32 = jnp.float32
    planes = doms // 2
    rows = 64 // planes
    vmem = pl.BlockSpec(memory_space=pltpu.VMEM)
    dma = pltpu.SemaphoreType.DMA
    moments, projected = pl.pallas_call(
        functools.partial(sweep_kernel, doms),
        out_shape=(pltpu.VMEM((512, NY), f32), pltpu.VMEM((16, 64, 64), f32)),
        in_specs=[pl.BlockSpec(memory_space=pl.ANY)] * 4,
        out_specs=(vmem, vmem),
        scratch_shapes=[
            pltpu.VMEM((2, 512, NY), f32),
            pltpu.VMEM((2, LINES, NY, NY), f32),
            pltpu.VMEM((2, NQ, NY), f32),
            pltpu.VMEM((2, LINES, NY, NY), f32),
            pltpu.VMEM((2, RIM, NY, NY), f32),
            pltpu.VMEM((2, 64, NY), f32),
            pltpu.VMEM((2, 64, NY), f32),
            pltpu.VMEM((2, 64, NY), f32),
            pltpu.VMEM((2, 64, NY), f32),
            pltpu.VMEM((2, 24, NY), f32),
            pltpu.VMEM((2, 24, NY), f32),
            pltpu.VMEM((2, 64, NY), f32),
            pltpu.VMEM((SPAN, NQ, NY), f32),
            pltpu.VMEM((SPAN, NQ, NY), f32),
            pltpu.VMEM((SPAN, 2, OWNED, NY), f32),
            pltpu.VMEM((SPAN, 16, NY), f32),
            pltpu.VMEM((20, 2 * NY, 2 * NY), jnp.bfloat16),
            pltpu.VMEM((20, 2 * NY, 2 * NY), jnp.bfloat16),
        ]
        + [pltpu.VMEM((SPAN, NQ * OWNED, NY), f32)] * 6
        + [pltpu.VMEM((NY, 2 * NY), f32)] * 3
        + [
            pltpu.VMEM((NY, NY), f32),
            pltpu.VMEM((planes, rows, NY), f32),
            pltpu.VMEM((planes, rows, NY), f32),
            pltpu.VMEM((16, rows, NY), f32),
            pltpu.VMEM((8, rows, NY), f32),
            pltpu.VMEM((planes, 8, rows, NY), f32),
        ]
        + [dma((5,))]
        + [dma((16,))] * 3
        + [dma((7,))] * 6
        + [dma((3,))] * 2
        + [dma((2,))] * 2
        + [dma((16,))] * 6,
        compiler_params=pltpu.CompilerParams(collective_id=0, has_side_effects=True, vmem_limit_bytes=60 * 1024 * 1024),
    )(probes.reshape(2, 512, NY), mass_weights, blocks, couplings.reshape(2, 48, NY))
    return moments.reshape(OWNED, MOM, 2, LINES, NY), projected.reshape(2, 8, 64, 64)


def solution(mesh):
    return jax.shard_map(
        functools.partial(on_device, mesh.shape["dom"]),
        mesh=mesh,
        in_specs=(P(None, None, "dom", None), P("dom", None), P(None, "dom", None, None), P(None, None, "dom", None)),
        out_specs=(P("quad", None, None, "dom", None), P()),
        check_vma=False,
    )
```

```python
import functools
import math

import jax
import jax.numpy as jnp
import numpy as np
from jax import lax
from jax.experimental import pallas as pl
from jax.experimental.pallas import tpu as pltpu
from jax.sharding import PartitionSpec as P

NQ = 16
MOM = 4
RADIUS = 2.0
OFFSETS = (-3, -2, -1, 1, 2, 3)
LINES = 8
OWNED = 8
NY = 128
FIRST = 9
SPAN = 26
ORDER = (7, 0, 6, 1, 5, 4, 3, 2)
RIM = 6
PLANE_ORDER = (10, 6, 9, 11, 14, 2, 8, 5, 7, 13, 3, 15, 1, 12, 4)
COLUMN_ORDER = (8, 7, 9, 6, 10, 5, 11, 4, 12, 3, 13, 2, 14, 15, 1)
NT = (((1,), (1,)), ((), ()))


def weights():
    theta = 2.0 * math.pi * (np.arange(NQ) + 0.5) / NQ
    return [[(RADIUS / NQ * math.cos(k * theta[a]), RADIUS / NQ * math.sin(k * theta[a])) for a in range(4)] for k in range(1, 2 * MOM + 1)]


WEIGHTS = weights()


def split(value):
    high = value.astype(jnp.bfloat16)
    low = (value - high.astype(jnp.float32)).astype(jnp.bfloat16)
    return high, low


def dot3(lhs, rhs_high, rhs_low):
    dot = functools.partial(lax.dot_general, dimension_numbers=NT, preferred_element_type=jnp.float32)
    high, low = split(lhs)
    count = lhs.shape[0]
    both = dot(jnp.concatenate([high, low], axis=0), rhs_high)
    return both[:count] + both[count:] + dot(high, rhs_low)


def sweep_kernel(
    doms, probes_hbm, mass_hbm, blocks_hbm, coup_hbm, mom_ref, out_ref,
    probes, blocks, table, zb, yb, zk, yk, pz, py, pe_own, pe_in, pack, inv_re, inv_im, src, cw, rhi, rlo,
    y1r, y1i, y2r, y2i, y3r, y3i, ima, imb, imc, gram, mine, gathered, column, total, full,
    in_sem, zs_send, zs_recv, zk_send, ys_send, ys_recv, sz_send, sz_recv, sy_send, sy_recv, ps_send, ps_recv, es_send, es_recv,
    s1, r1, s2, r2, s3, r3,
):
    q = lax.axis_index("quad")
    d = lax.axis_index("dom")
    c = lax.rem(q, 2)
    o = 1 - c
    zl = lax.div(q, 2)
    zh = lax.rem(d, 2)
    flip = d + 1 - 2 * zh
    up = lax.rem(d + 2, doms)
    down = lax.rem(d + doms - 2, doms)
    y_to = lax.rem(d + 2 - 4 * zh + doms, doms)
    at_top = lax.div(q + 2, 8)
    at_bottom = 1 - lax.div(q + 6, 8)
    head = (1 - c) * at_top + c * at_bottom
    q_to = lax.rem(q + 8 + 2 - 4 * c, 8)
    d_to = d + head * (1 - 2 * zh)
    sib = q + 1 - 2 * c
    mirror = 2 * (3 - zl) + c
    is_head = head == 1
    depth = c * (3 - zl) + (1 - c) * zl
    far = lax.div(depth, 2) == 1
    q_skip = lax.rem(q + 8 + 4 - 8 * c, 8)
    planes = doms // 2
    rows = 64 // planes
    m = lax.div(d, 2)
    slot = zh * 8 + q

    arrivals = [
        pltpu.make_async_copy(coup_hbm, pack.at[:, pl.ds(0, 48), :], in_sem.at[0]),
        pltpu.make_async_copy(mass_hbm, pack.at[0, pl.ds(56, 8), :], in_sem.at[1]),
        pltpu.make_async_copy(mass_hbm, pack.at[1, pl.ds(56, 8), :], in_sem.at[2]),
        pltpu.make_async_copy(probes_hbm, probes, in_sem.at[3]),
        pltpu.make_async_copy(blocks_hbm, blocks, in_sem.at[4]),
    ]
    for arrival in arrivals:
        arrival.start()

    barrier = pltpu.get_barrier_semaphore()

    def greet(quad, dom):
        pl.semaphore_signal(barrier, inc=1, device_id={"quad": quad, "dom": dom}, device_id_type=pl.DeviceIdType.MESH)

    @pl.loop(1, planes)
    def _(i):
        greet(q, lax.rem(m + i, planes) * 2 + zh)

    @pl.loop(1, 16)
    def _(i):
        to = lax.rem(slot + i, 16)
        greet(lax.rem(to, 8), 2 * m + lax.div(to, 8))

    def copy(source, target, send, recv, quad, dom):
        return pltpu.make_async_remote_copy(
            src_ref=source, dst_ref=target, send_sem=send, recv_sem=recv,
            device_id={"quad": quad, "dom": dom}, device_id_type=pl.DeviceIdType.MESH,
        )

    def z_copy(s):
        t = ORDER[s // 2]
        piece = zb.at[c, t, pl.ds(s % 2 * 64, 64), :]
        return copy(piece, piece, zs_send.at[s], zs_recv.at[s], q_to, d_to)

    def z_skip(s):
        t = ORDER[s // 2]
        piece = zb.at[c, t, pl.ds(s % 2 * 64, 64), :]
        return copy(piece, piece, zk_send.at[s], zs_recv.at[s], q_skip, d)

    def z_head(s):
        t = ORDER[s // 2]
        half = pl.ds(s % 2 * 64, 64)
        line = zh * t + (1 - zh) * (LINES - 1 - t)
        return copy(blocks_hbm.at[c, line, half, :], zb.at[c, t, half, :], zs_send.at[s], zs_recv.at[s], q_to, d_to)

    def y_pack():
        return copy(zk.at[c], yk.at[c], ys_send.at[RIM], ys_recv.at[RIM], q, y_to)

    def y_copy(u):
        return copy(zb.at[c, LINES - 1 - u], yb.at[c, u], ys_send.at[u], ys_recv.at[u], q, y_to)

    def sz_pack(part):
        return copy(zk.at[part], zk.at[part], sz_send.at[RIM], sz_recv.at[RIM], sib, d)

    def sz_copy(t, part):
        return copy(zb.at[part, t], zb.at[part, t], sz_send.at[t], sz_recv.at[t], sib, d)

    def sy_pack(part):
        return copy(yk.at[part], yk.at[part], sy_send.at[RIM], sy_recv.at[RIM], sib, d)

    def sy_copy(u, part):
        return copy(yb.at[part, u], yb.at[part, u], sy_send.at[u], sy_recv.at[u], sib, d)

    k_mirror = copy(pack.at[c], zk.at[c], ps_send.at[2], ps_recv.at[2], mirror, flip)
    p_mirror = copy(probes_hbm.at[:, pl.ds(mirror * OWNED * LINES, OWNED * LINES), :], pz, ps_send.at[0], ps_recv.at[0], mirror, flip)
    p_next = copy(pz, py, ps_send.at[1], ps_recv.at[1], q, y_to)
    e_up = copy(pe_own.at[1], pe_in.at[1], es_send.at[1], es_recv.at[1], q, up)
    e_down = copy(pe_own.at[0], pe_in.at[0], es_send.at[0], es_recv.at[0], q, down)

    eye = lax.broadcasted_iota(jnp.int32, (NY, NY), 0) == lax.broadcasted_iota(jnp.int32, (NY, NY), 1)

    row = lax.broadcasted_iota(jnp.int32, (NQ, NY), 0)
    for part, function in ((0, math.cos), (1, math.sin)):
        values = jnp.zeros((NQ, NY), jnp.float32)
        for j in range(NQ):
            values = jnp.where(row == j, RADIUS * function(2.0 * math.pi * (j + 0.5) / NQ), values)
        table[part] = values
    for arrival in arrivals:
        arrival.wait()

    @pl.loop(0, LINES)
    def _(line):
        for part in range(2):
            diagonal = jnp.sum(jnp.where(eye, blocks[part, line], 0.0), axis=0, keepdims=True)
            pack[part, pl.ds(48 + line, 1), :] = diagonal

    for side, line in ((0, 0), (1, LINES - 1)):
        for part in range(2):
            pe_own[side, 8 * part : 8 * part + 8, :] = probes[part, pl.ds(q * OWNED * LINES + line, OWNED, stride=LINES), :]
            pe_own[side, 17 + part : 18 + part, :] = pack[part, 48 + line : 49 + line, :]
        pe_own[side, 16:17, :] = pack[0, 56 + line : 57 + line, :]

    pl.semaphore_wait(barrier, planes - 1 + 15)

    @pl.when(is_head)
    def _():
        for s in range(2 * len(ORDER)):
            z_head(s).start()

    k_mirror.start()
    p_mirror.start()
    e_up.start()
    e_down.start()

    def prepare(w, probe_re, probe_im, weight, diag_re, diag_im):
        line = d * LINES + zh * (w - FIRST) + (1 - zh) * (SPAN - 1 - FIRST - w)
        inside = jnp.logical_and(line >= 0, line < doms * LINES)
        source_re = weight * probe_re
        source_im = weight * probe_im
        src[w, 0] = source_re
        src[w, 1] = source_im
        denom_re = table[0] * weight - diag_re
        denom_im = table[1] * weight - diag_im
        modulus = denom_re * denom_re + denom_im * denom_im
        inv_re[w] = jnp.where(inside, denom_re / modulus, 0.0)
        inv_im[w] = jnp.where(inside, -denom_im / modulus, 0.0)
        for j in range(NQ):
            g_re = inv_re[w, j : j + 1, :]
            g_im = inv_im[w, j : j + 1, :]
            y1r[w, 8 * j : 8 * j + 8, :] = source_re * g_re - source_im * g_im
            y1i[w, 8 * j : 8 * j + 8, :] = source_re * g_im + source_im * g_re

    def couple(w, ref, line):
        for position in range(6):
            row = zh * position + (1 - zh) * (5 - position)
            for part in range(2):
                cw[w, 6 * part + position : 6 * part + position + 1, :] = ref[part, pl.ds(row * LINES + line, 1), :]

    def prepare_packed(w, line, probe, packed):
        couple(w, packed, line)
        prepare(
            w,
            probe[0, pl.ds(line, OWNED, stride=LINES), :],
            probe[1, pl.ds(line, OWNED, stride=LINES), :],
            packed[0, pl.ds(56 + line, 1), :],
            packed[0, pl.ds(48 + line, 1), :],
            packed[1, pl.ds(48 + line, 1), :],
        )

    def prepare_edge(w, side):
        prepare(w, pe_in[side, 0:8, :], pe_in[side, 8:16, :], pe_in[side, 16:17, :], pe_in[side, 17:18, :], pe_in[side, 18:19, :])

    def own_line(w):
        return zh * (w - FIRST) + (1 - zh) * (SPAN - 1 - FIRST - w)

    def operand(w, block_re, block_im):
        re_high, re_low = split(jnp.where(eye, 0.0, block_re))
        im_high, im_low = split(jnp.where(eye, 0.0, block_im))
        for ref, re, im in ((rhi, re_high, im_high), (rlo, re_low, im_low)):
            ref[w - 3, 0:NY, 0:NY] = re
            ref[w - 3, 0:NY, NY:] = -im
            ref[w - 3, NY:, 0:NY] = im
            ref[w - 3, NY:, NY:] = re

    def image(yr, yi, w, into):
        into[...] = dot3(jnp.concatenate([yr[w], yi[w]], axis=1), rhi[w - 3], rlo[w - 3])

    def finish(yr, yi, w, image_ref, emit, order=range(NQ)):
        c_re = [cw[w, i : i + 1, :] for i in range(6)]
        c_im = [cw[w, 6 + i : 7 + i, :] for i in range(6)]
        source_re = src[w, 0]
        source_im = src[w, 1]
        for j in order:
            part = slice(8 * j, 8 * j + 8)
            a_re = image_ref[part, :NY] + source_re
            a_im = image_ref[part, NY:] + source_im
            for i, offset in enumerate(OFFSETS):
                n_re = yr[w + offset, part, :]
                n_im = yi[w + offset, part, :]
                a_re = a_re + (c_re[i] * n_re - c_im[i] * n_im)
                a_im = a_im + (c_re[i] * n_im + c_im[i] * n_re)
            g_re = inv_re[w, j : j + 1, :]
            g_im = inv_im[w, j : j + 1, :]
            emit(j, g_re * a_re - g_im * a_im, g_re * a_im + g_im * a_re)

    def keep(yr, yi, w):
        def emit(j, re, im):
            yr[w, 8 * j : 8 * j + 8, :] = re
            yi[w, 8 * j : 8 * j + 8, :] = im

        return emit

    def second(w, image_ref):
        finish(y1r, y1i, w, image_ref, keep(y2r, y2i, w))

    def third(w, image_ref):
        finish(y2r, y2i, w, image_ref, keep(y3r, y3i, w))

    def last(w, image_ref):
        line = own_line(w)
        field = {}

        def emit(j, re, im):
            field[j] = (re, im)

        finish(y3r, y3i, w, image_ref, emit, [a + 4 * b for a in range(4) for b in range(4)])
        sum_re = [None] * (2 * MOM)
        sum_im = [None] * (2 * MOM)
        for a in range(4):
            (r0, i0), (r1, i1), (r2, i2), (r3, i3) = (field[a + 4 * b] for b in range(4))
            er, ei, fr, fi = r0 + r2, i0 + i2, r0 - r2, i0 - i2
            gr, gi, hr, hi = r1 + r3, i1 + i3, r1 - r3, i1 - i3
            groups = ((er + gr, ei + gi), (fr - hi, fi + hr), (er - gr, ei - gi), (fr + hi, fi - hr))
            for k in range(2 * MOM):
                x_re, x_im = groups[(k + 1) % 4]
                w_re, w_im = WEIGHTS[k][a]
                t_re = w_re * x_re - w_im * x_im
                t_im = w_re * x_im + w_im * x_re
                sum_re[k] = t_re if a == 0 else sum_re[k] + t_re
                sum_im[k] = t_im if a == 0 else sum_im[k] + t_im
        for k in range(MOM):
            mom_ref[pl.ds(k * 16 + line, OWNED, stride=64), :] = sum_re[k]
            mom_ref[pl.ds(k * 16 + 8 + line, OWNED, stride=64), :] = sum_im[k]
        m_high, m_low = split(jnp.concatenate(sum_re + sum_im, axis=0))
        probe_lines = jnp.concatenate([probes[part, pl.ds(line, 64, stride=LINES), :] for part in range(2)], axis=0)
        gram[...] += dot3(probe_lines, m_high, m_low)

    def pairs(yr, yi, step, first, count):
        image(yr, yi, first, ima)

        @pl.loop(0, count // 2)
        def _(i):
            w = first + 2 * i
            image(yr, yi, w + 1, imb)
            step(w, ima)
            image(yr, yi, jnp.minimum(w + 2, first + count - 1), ima)
            step(w + 1, imb)

        if count % 2:
            step(first + count - 1, ima)

    def relay(s):
        for piece in (2 * s, 2 * s + 1):
            z_copy(piece).wait_recv()
            first = z_skip(piece), z_copy(piece)

            @pl.when(depth == 0)
            def _():
                first[0].start()
                first[1].start()

            pl.when(depth == 2)(first[1].start)

        if ORDER[s] >= 2:
            y_copy(LINES - 1 - ORDER[s]).start()

        if ORDER[s] < RIM:
            sz_copy(ORDER[s], c).start()

    def pass_small():
        k_mirror.wait_recv()
        y_pack().start()
        sz_pack(c).start()
        p_mirror.wait_recv()
        p_next.start()

    def prepare_z():
        sz_pack(o).wait_recv()
        e_down.wait_recv()
        e_up.wait_recv()

        @pl.loop(0, LINES)
        def _(t):
            prepare_packed(FIRST - 1 - t, (1 - zh) * t + zh * (LINES - 1 - t), pz, zk)

        prepare_edge(0, zh)

    def share_y():
        y_pack().wait_recv()
        sy_pack(c).start()

    def prepare_y():
        p_next.wait_recv()
        sy_pack(o).wait_recv()

        @pl.loop(0, LINES)
        def _(u):
            prepare_packed(FIRST + LINES + u, (1 - zh) * (LINES - 1 - u) + zh * u, py, yk)

        prepare_edge(SPAN - 1, 1 - zh)

    gram[...] = jnp.zeros_like(gram)

    @pl.loop(FIRST, FIRST + LINES)
    def _(w):
        line = own_line(w)
        couple(w, pack, line)
        prepare(
            w,
            probes[0, pl.ds(q * OWNED * LINES + line, OWNED, stride=LINES), :],
            probes[1, pl.ds(q * OWNED * LINES + line, OWNED, stride=LINES), :],
            pack[0, pl.ds(56 + line, 1), :],
            pack[0, pl.ds(48 + line, 1), :],
            pack[1, pl.ds(48 + line, 1), :],
        )
        operand(w, blocks[0, line], blocks[1, line])

    def z_pair(t):
        w = FIRST - 1 - t
        sz_copy(t, o).wait_recv()
        operand(w, zb[0, t], zb[1, t])
        image(y1r, y1i, w, ima)
        sz_copy(t + 1, o).wait_recv()
        operand(w - 1, zb[0, t + 1], zb[1, t + 1])
        image(y1r, y1i, w - 1, imb)
        second(w, ima)
        second(w - 1, imb)

    def share(u):
        y_copy(u).wait_recv()
        sy_copy(u, c).start()

    def y_line(u):
        sy_copy(u, o).wait_recv()
        w = FIRST + LINES + u
        image(y2r, y2i, w - 3, imb)
        operand(w, yb[0, u], yb[1, u])
        image(y1r, y1i, w, ima)
        second(w, ima)
        third(w - 3, imb)

    own = functools.partial(pairs, y1r, y1i, second)

    @pl.when(jnp.logical_not(far))
    def _():
        for s in range(4):
            relay(s)
        pass_small()
        relay(4)
        prepare_z()
        relay(5)
        own(FIRST, 2)
        relay(6)
        own(FIRST + 2, 2)
        relay(7)
        share_y()
        prepare_y()
        own(FIRST + 4, 4)
        for u in range(3):
            share(u)
        z_pair(0)
        pairs(y2r, y2i, third, FIRST + 1, 4)
        pl.loop(0, 2)(y_line)
        for u in range(3, RIM):
            share(u)
        z_pair(4)
        y_line(2)

    @pl.when(jnp.logical_and(far, head == 0))
    def _():
        relay(0)
        relay(1)
        pass_small()
        relay(2)
        prepare_z()
        relay(3)
        own(FIRST, 2)
        relay(4)
        own(FIRST + 2, 2)
        relay(5)
        share_y()
        relay(6)
        relay(7)
        prepare_y()
        share(0)
        share(1)
        own(FIRST + 4, 4)
        z_pair(0)
        share(2)
        pairs(y2r, y2i, third, FIRST + 1, 4)
        z_pair(4)
        pl.loop(0, 3)(y_line)

    @pl.when(is_head)
    def _():
        pass_small()
        prepare_z()
        own(FIRST, 4)
        relay(0)
        relay(1)
        share_y()
        relay(2)
        prepare_y()
        relay(3)
        own(FIRST + 4, 4)
        relay(4)
        share(0)
        z_pair(0)
        relay(5)
        pairs(y2r, y2i, third, FIRST + 1, 4)
        relay(6)
        share(1)
        z_pair(4)
        y_line(0)
        relay(7)
        share(2)
        pl.loop(1, 3)(y_line)

    pl.when(far)(functools.partial(share, 3))
    z_pair(2)
    pairs(y2r, y2i, third, FIRST - 3, 4)
    pairs(y3r, y3i, last, FIRST, 5)

    @pl.loop(3, RIM)
    def _(u):
        @pl.when(jnp.logical_and(far, u < RIM - 1))
        def _():
            y_copy(u + 1).wait_recv()
            sy_copy(u + 1, c).start()

        sy_copy(u, o).wait_recv()
        w = FIRST + LINES + u
        image(y3r, y3i, w - 6, imc)
        image(y2r, y2i, w - 3, imb)
        operand(w, yb[0, u], yb[1, u])
        image(y1r, y1i, w, ima)
        second(w, ima)
        third(w - 3, imb)
        last(w - 6, imc)

    lane = lax.broadcasted_iota(jnp.int32, (64, 128), 1)
    other = pltpu.roll(gram[64:, :], 64, 1)
    scale = 1.0 / float(doms * LINES * NY)
    partial = scale * (gram[:64, :] + jnp.where(lane < 64, other, -other))
    for i in range(planes):
        mine[i] = partial[i * rows : (i + 1) * rows, :]

    def dev(quad, dom):
        return {"quad": quad, "dom": dom}

    def plane_copy(i):
        to = lax.rem(m + i, planes)
        return pltpu.make_async_remote_copy(
            src_ref=mine.at[to], dst_ref=gathered.at[i], send_sem=s1.at[i], recv_sem=r1.at[i],
            device_id=dev(q, to * 2 + zh), device_id_type=pl.DeviceIdType.MESH,
        )

    def column_copy(i):
        to = lax.rem(slot + i, 16)
        return pltpu.make_async_remote_copy(
            src_ref=column.at[slot], dst_ref=column.at[slot], send_sem=s2.at[i], recv_sem=r2.at[i],
            device_id=dev(lax.rem(to, 8), 2 * m + lax.div(to, 8)), device_id_type=pl.DeviceIdType.MESH,
        )

    def column_arrived(i):
        come = lax.rem(slot + 16 - i, 16)
        return pltpu.make_async_remote_copy(
            src_ref=column.at[come], dst_ref=column.at[come], send_sem=s2.at[i], recv_sem=r2.at[i],
            device_id=dev(lax.rem(come, 8), 2 * m + lax.div(come, 8)), device_id_type=pl.DeviceIdType.MESH,
        )

    def full_copy(i):
        to = lax.rem(m + i, planes)
        return pltpu.make_async_remote_copy(
            src_ref=total, dst_ref=full.at[m], send_sem=s3.at[i], recv_sem=r3.at[m],
            device_id=dev(q, to * 2 + zh), device_id_type=pl.DeviceIdType.MESH,
        )

    def full_arrived(come):
        return pltpu.make_async_remote_copy(
            src_ref=total, dst_ref=full.at[come], send_sem=s3.at[come], recv_sem=r3.at[come],
            device_id=dev(q, come * 2 + zh), device_id_type=pl.DeviceIdType.MESH,
        )

    for i in PLANE_ORDER:
        plane_copy(i).start()

    gathered[0] = mine[m]

    for i in range(1, planes):
        plane_copy(i).wait_recv()

    column[slot] = functools.reduce(lambda a, b: a + b, [gathered[i] for i in range(planes)])

    for i in COLUMN_ORDER:
        column_copy(i).start()

    for i in range(1, 16):
        column_arrived(i).wait_recv()

    group = lax.div(lax.broadcasted_iota(jnp.int32, (rows, NY), 1), 8)
    sums = [column[i] + column[8 + i] for i in range(8)]
    for pair in range(8):
        value = jnp.zeros((rows, NY), jnp.float32)
        for half in range(2):
            for i in range(8):
                to = 8 * half + i
                shift = (to - 2 * pair - half) % 16 * 8
                moved = pltpu.roll(sums[i], shift, 1) if shift else sums[i]
                value = jnp.where(group == to, moved, value)
        total[pair] = value

    for i in PLANE_ORDER:
        full_copy(i).start()

    full[m] = total[...]

    for i in range(planes):
        pl.when(m != i)(full_arrived(i).wait_recv)
        for pair in range(8):
            value = full[i, pair]
            out_ref[2 * pair, rows * i : rows * (i + 1), :] = value[:, :64]
            out_ref[2 * pair + 1, rows * i : rows * (i + 1), :] = value[:, 64:]

    @pl.loop(1, planes)
    def _(i):
        plane_copy(i).wait_send()
        full_copy(i).wait_send()

    @pl.loop(1, 16)
    def _(i):
        column_copy(i).wait_send()

    k_mirror.wait_send()
    p_mirror.wait_send()
    p_next.wait_send()
    e_up.wait_send()
    e_down.wait_send()

    @pl.when(depth != 1)
    def _():
        for s in range(2 * len(ORDER)):
            z_copy(s).wait_send()

    @pl.when(depth == 0)
    def _():
        for s in range(2 * len(ORDER)):
            z_skip(s).wait_send()

    y_pack().wait_send()
    sz_pack(c).wait_send()
    sy_pack(c).wait_send()
    for i in range(RIM):
        y_copy(i).wait_send()
        sz_copy(i, c).wait_send()
        sy_copy(i, c).wait_send()


def on_device(doms, probes, mass_weights, blocks, couplings):
    f32 = jnp.float32
    planes = doms // 2
    rows = 64 // planes
    vmem = pl.BlockSpec(memory_space=pltpu.VMEM)
    dma = pltpu.SemaphoreType.DMA
    moments, projected = pl.pallas_call(
        functools.partial(sweep_kernel, doms),
        out_shape=(pltpu.VMEM((512, NY), f32), pltpu.VMEM((16, 64, 64), f32)),
        in_specs=[pl.BlockSpec(memory_space=pl.ANY)] * 4,
        out_specs=(vmem, vmem),
        scratch_shapes=[
            pltpu.VMEM((2, 512, NY), f32),
            pltpu.VMEM((2, LINES, NY, NY), f32),
            pltpu.VMEM((2, NQ, NY), f32),
            pltpu.VMEM((2, LINES, NY, NY), f32),
            pltpu.VMEM((2, RIM, NY, NY), f32),
            pltpu.VMEM((2, 64, NY), f32),
            pltpu.VMEM((2, 64, NY), f32),
            pltpu.VMEM((2, 64, NY), f32),
            pltpu.VMEM((2, 64, NY), f32),
            pltpu.VMEM((2, 24, NY), f32),
            pltpu.VMEM((2, 24, NY), f32),
            pltpu.VMEM((2, 64, NY), f32),
            pltpu.VMEM((SPAN, NQ, NY), f32),
            pltpu.VMEM((SPAN, NQ, NY), f32),
            pltpu.VMEM((SPAN, 2, OWNED, NY), f32),
            pltpu.VMEM((SPAN, 16, NY), f32),
            pltpu.VMEM((20, 2 * NY, 2 * NY), jnp.bfloat16),
            pltpu.VMEM((20, 2 * NY, 2 * NY), jnp.bfloat16),
        ]
        + [pltpu.VMEM((SPAN, NQ * OWNED, NY), f32)] * 6
        + [pltpu.VMEM((NY, 2 * NY), f32)] * 3
        + [
            pltpu.VMEM((NY, NY), f32),
            pltpu.VMEM((planes, rows, NY), f32),
            pltpu.VMEM((planes, rows, NY), f32),
            pltpu.VMEM((16, rows, NY), f32),
            pltpu.VMEM((8, rows, NY), f32),
            pltpu.VMEM((planes, 8, rows, NY), f32),
        ]
        + [dma((5,))]
        + [dma((16,))] * 3
        + [dma((7,))] * 6
        + [dma((3,))] * 2
        + [dma((2,))] * 2
        + [dma((16,))] * 6,
        compiler_params=pltpu.CompilerParams(collective_id=0, has_side_effects=True, vmem_limit_bytes=60 * 1024 * 1024),
    )(probes.reshape(2, 512, NY), mass_weights, blocks, couplings.reshape(2, 48, NY))
    return moments.reshape(OWNED, MOM, 2, LINES, NY), projected.reshape(2, 8, 64, 64)


def solution(mesh):
    return jax.shard_map(
        functools.partial(on_device, mesh.shape["dom"]),
        mesh=mesh,
        in_specs=(P(None, None, "dom", None), P("dom", None), P(None, "dom", None, None), P(None, None, "dom", None)),
        out_specs=(P("quad", None, None, "dom", None), P()),
        check_vma=False,
    )
```
